32 devices in a mesh: inst: 8 (over y, x, core), tp: 4 (over z).
Axes of the slice: x: 2, y: 2, z: 4, core: 2. Of those that a mesh axis runs over, the one named last changes fastest.
Arguments:
- source_cache: bfloat16 [8, 4, 2, 512, 1024], P('inst', 'tp'), may hold values from -6 to 6
- resident_cache: bfloat16 [8, 4, 8, 2, 512, 256], P('inst', 'tp'), may hold values from -6 to 6
- new_kv: bfloat16 [8, 12, 2, 1024], P('inst'), may hold values from -6 to 6
- queries: bfloat16 [8, 12, 4096], P('inst', None, 'tp'), may hold values from -103 to 103
- residual: bfloat16 [8, 12, 8192], P('inst'), may hold values from -1.5 to 1.5
- lengths: int32 [8, 12], P('inst'), may hold values from 1 to 512, 3072 in all within a row
- out_weight: bfloat16 [4096, 8192], P('tp'), may hold values from -0.09375 to 0.09375
Outputs:
- mixed: bfloat16 [8, 12, 8192], P('inst')
- adopted_cache: bfloat16 [8, 4, 4, 2, 512, 256], P('inst', 'tp')
The draws below stay inside these ranges and needn't reach their ends.
All inputs are finite; a program needn't handle non-finite values.
Results may differ from the reference program's by a relative error of at most 0.0052.
Values may be sent and summed in bfloat16 or wider, within the bound.
A program may use at most 64 MiB of HBM per device.

```python
import math
import jax
import jax.numpy as jnp
import numpy as np
from jax import lax

D = 8192
HD = 128
KVH = 8
QH = 32
LEN = 512
RES = 8
ADOPT = 4
ROWS = 12
KV_DEV = 2
N_INST = 8
N_TP = 4


def draw_queries(key, part):
    key = jax.random.fold_in(key, 7)
    first_key = jax.random.fold_in(key, 0)
    values = jnp.clip(2.0 * jax.random.normal(first_key, (N_INST, ROWS, QH * HD), jnp.float32), -12.0, 12.0)
    return values.astype(jnp.bfloat16)


def block_scale(rng, extent, pieces, least, top_value):
    gain, own = 1.0, jax.random.fold_in(rng, 6)
    for dim, blocks in pieces:
        steps = jnp.exp(jax.random.uniform(jax.random.fold_in(own, dim), (blocks,), jnp.float32, least / len(pieces), top_value / len(pieces)))
        gain = gain * jnp.repeat(steps, extent[dim] // blocks).reshape([-1 if axis == dim else 1 for axis in range(len(extent))])
    return gain


def split_up(number_of, total, bound, skew):
    weights = [(1 << 20) // math.isqrt(grade ** skew) + 1 for grade in range(2, number_of + 1)]
    rest, counts = total - bound - (number_of - 1), [1] * (number_of - 1)
    while rest > 0:
        free = [i for i in range(number_of - 1) if counts[i] < bound]
        whole, remaining = sum([weights[i] for i in free]), rest
        for i in free:
            more = min(bound - counts[i], max(1, remaining * weights[i] // whole), rest)
            counts[i] = counts[i] + more
            rest = rest - more
    return np.array([bound] + counts)


def uneven_parts(own_key, count, total, limit, slope):
    if count == 2:
        one = jax.random.randint(own_key, (), max(1, total - limit), min(limit, total - 1) + 1)
        return jnp.stack([one, total - one])
    sizes = jnp.asarray(split_up(count, total, limit, slope), jnp.int32)
    twos = (count - 1) // 2
    giver, taker = sizes[1:1 + 2 * twos:2], sizes[2:2 + 2 * twos:2]
    slack = jnp.minimum(giver - 1, limit - taker)
    shifted = jax.random.randint(jax.random.fold_in(own_key, 1), (twos,), 0, 1 << 20) % (slack + 1)
    sizes = sizes.at[1:1 + 2 * twos:2].set(giver - shifted).at[2:2 + 2 * twos:2].set(taker + shifted)
    return sizes[jax.random.permutation(jax.random.fold_in(own_key, 2), count)]


def centred(stream_key, dims, spread, limit, pieces=(), kind=jnp.bfloat16):
    entries = jax.random.normal(stream_key, dims, jnp.float32) * spread
    if len(pieces) > 0:
        entries = block_scale(stream_key, dims, pieces, -0.22, 0.18) * entries
    return jnp.clip(entries, min=-limit, max=limit).astype(kind)


def setup_inputs(seed: int = 0) -> dict:
    splits = jax.random.split(jax.random.key(seed), 8)
    source_cache = centred(splits[0], (N_INST, ADOPT, 2, LEN, KVH * HD), 1.0, 6.0, ((0, 8), (1, 4)))
    resident_cache = centred(splits[1], (N_INST, N_TP, RES, 2, LEN, KV_DEV * HD), 1.0, 6.0, ((0, 8), (1, 4)))
    new_kv = centred(splits[2], (N_INST, ROWS, 2, KVH * HD), 1.0, 6.0, ((0, 8),))
    queries = draw_queries(jax.random.fold_in(splits[7], 71), 0)
    residual = centred(splits[4], (N_INST, ROWS, D), 0.25, 1.5, ((0, 8),))
    lengths = jax.vmap(lambda own: uneven_parts(own, ROWS, ROWS * LEN // 2, LEN, 1))(jax.random.split(splits[5], N_INST)).reshape((N_INST, ROWS)).astype(jnp.int32)
    out_weight = centred(splits[6], (QH * HD, D), (QH * HD) ** -0.5, 0.09375, ((0, 4),))
    return dict(source_cache=source_cache, resident_cache=resident_cache, new_kv=new_kv, queries=queries, residual=residual, lengths=lengths, out_weight=out_weight)


def attend(query_vector, key_cache, value_cache, incoming_key, value_fresh, seq_lengths):
    softmax_scale = 1.0 / math.sqrt(query_vector.shape[-1])
    query_broadcast = query_vector.astype(jnp.float32)
    scores = jnp.einsum('bkgd,blkd->bkgl', query_broadcast, key_cache.astype(jnp.float32)) * softmax_scale
    local_score = jnp.einsum('heox,hex->heo', query_broadcast, incoming_key.astype(jnp.float32)) * softmax_scale
    places = jnp.arange(key_cache.shape[1], dtype=jnp.int32)
    live_mask = (places[None, :] < seq_lengths[:, None])[:, None, None, :]
    scores = jnp.where(live_mask, scores, -1e+30)
    top_score = jnp.maximum(lax.optimization_barrier(jnp.max(scores, axis=-1)), local_score)
    weights = jnp.where(live_mask, jnp.exp(scores - top_score[..., None]), 0.0)
    local_weight = jnp.exp(local_score - top_score)
    total = lax.optimization_barrier(jnp.sum(weights, axis=-1)) + local_weight
    probs = lax.optimization_barrier((weights / total[..., None]).astype(jnp.bfloat16))
    own_prob = lax.optimization_barrier((local_weight / total).astype(jnp.bfloat16))
    blended = jnp.einsum('bkgl,blkd->bkgd', probs.astype(jnp.float32), value_cache.astype(jnp.float32))
    blended = blended + own_prob.astype(jnp.float32)[..., None] * value_fresh.astype(jnp.float32)[:, :, None, :]
    return blended.reshape(blended.shape[0], -1).astype(jnp.bfloat16)

def reference(source_cache, resident_cache, new_kv, queries, residual, lengths, out_weight):
    half_way = N_INST // 2
    handed = jnp.roll(source_cache, half_way, axis=0)
    handed_len = jnp.roll(lengths[:, :ADOPT], half_way, axis=0)
    own_len = lengths[:, ADOPT:]
    group = QH // KVH
    per_dev = QH // N_TP
    kv_dev = max(1, per_dev // group)
    per_kv = per_dev // kv_dev
    head_table = np.array([[dev * per_dev // group + slot for slot in range(kv_dev)] for dev in range(N_TP)], dtype=np.int32)
    split_heads = handed.reshape(N_INST, ADOPT, 2, LEN, KVH, HD)[:, :, :, :, head_table]
    adopted_cache = jnp.transpose(split_heads, (0, 4, 1, 2, 3, 5, 6)).reshape(N_INST, N_TP, ADOPT, 2, LEN, kv_dev * HD)

    def one_instance(items):
        cache, resident, fresh, query_vector, resid, res_len, hand_len = items
        fresh = fresh.reshape(ROWS, 2, KVH, HD)
        query_heads = query_vector.reshape(ROWS, QH, HD)
        query_adopt = query_heads[:ADOPT].reshape(ADOPT, KVH, group, HD)
        cache_heads = cache.reshape(ADOPT, 2, LEN, KVH, HD)
        out_adopt = attend(query_adopt, cache_heads[:, 0], cache_heads[:, 1], fresh[:ADOPT, 0], fresh[:ADOPT, 1], hand_len)
        query_res = query_heads[ADOPT:].reshape(RES * N_TP, kv_dev, per_kv, HD)
        resident_rows = jnp.transpose(resident, (1, 0, 2, 3, 4)).reshape(RES * N_TP, 2, LEN, kv_dev, HD)
        fresh_res = fresh[ADOPT:][:, :, head_table]
        fresh_res = jnp.transpose(fresh_res, (0, 2, 1, 3, 4)).reshape(RES * N_TP, 2, kv_dev, HD)
        out_res = attend(query_res, resident_rows[:, 0], resident_rows[:, 1], fresh_res[:, 0], fresh_res[:, 1], jnp.repeat(res_len, N_TP))
        out_res = out_res.reshape(RES, QH * HD)
        attn = jnp.concatenate([out_adopt, out_res], axis=0)
        value_portion = jnp.dot(attn, out_weight, preferred_element_type=jnp.float32)
        return (resid.astype(jnp.float32) + value_portion).astype(jnp.bfloat16)
    mixed = lax.map(one_instance, (handed, resident_cache, new_kv, queries, residual, own_len, handed_len))
    return (mixed, adopted_cache)
```

```python
import functools
import math

import jax
import jax.numpy as jnp
from jax import lax
from jax.experimental import pallas as pl
from jax.experimental.pallas import tpu as pltpu
from jax.sharding import PartitionSpec as P

HD = 128
KVH = 8
QH = 32
TILE = 16
MESH = pl.DeviceIdType.MESH
BF16 = jnp.bfloat16
F32 = jnp.float32


def fold(value, rows):
    pieces = max(1, TILE // rows)
    width = value.shape[1] // pieces
    return jnp.concatenate(
        [value[:, j * width : (j + 1) * width] for j in range(pieces)], axis=0
    )


def kernel(
    dims,
    source_ref, resident_ref, newkv_ref, query_ref, resid_ref, lens_ref, weight_ref,
    mixed_ref, adopted_ref,
    cache, resident, weight, q_raw, nk_raw, rs_raw, len_raw, len_in,
    qf, nkf, resf, attn_a, attn_b, prob, own_prob,
    send_a, land_a, all_a, send_b, land_b, all_b, total_a, total_b,
    kv_send, kv_recv, len_sem, load_sem, out_sem,
    rs_send_a, rs_recv_a, ag_send_a, ag_recv_a,
    rs_send_b, rs_recv_b, ag_send_b, ag_recv_b,
):
    n_inst, n_tp, adopt, res_rows, kv_dev, per_kv, span = dims
    per_dev = kv_dev * per_kv
    group = QH // KVH
    wide = kv_dev * HD
    inst, tp = lax.axis_index("inst"), lax.axis_index("tp")
    other = lax.rem(inst + n_inst // 2, n_inst)
    scale = 1.0 / math.sqrt(HD)
    model = weight_ref.shape[1]
    share = model // n_tp

    def column(rank):
        return pl.multiple_of((rank * per_dev) // group * HD, HD)

    barrier = pltpu.get_barrier_semaphore()
    for o in range(n_tp):
        pl.semaphore_signal(barrier, inc=1, device_id=(other, lax.rem(tp + o, n_tp)), device_id_type=MESH)
        if o > 0:
            pl.semaphore_signal(barrier, inc=1, device_id=(inst, lax.rem(tp + o, n_tp)), device_id_type=MESH)
    pl.semaphore_wait(barrier, 2 * n_tp - 1)

    core = lax.rem(inst, 2)

    def handoff(which, k):
        base = (k // 2 + (n_tp // 2 if k % 2 == 0 else 0)) % n_tp
        rank = lax.rem(tp + base + core * (n_tp // 2), n_tp)
        return pltpu.make_async_remote_copy(
            src_ref=source_ref.at[0, 0, which, :, pl.ds(column(rank), wide)],
            dst_ref=cache.at[tp, which],
            send_sem=kv_send.at[which, k],
            recv_sem=kv_recv.at[which, tp],
            device_id=(other, rank),
            device_id_type=MESH,
        )

    def arrived(which, row):
        pltpu.make_async_remote_copy(
            src_ref=cache.at[row, which],
            dst_ref=cache.at[row, which],
            send_sem=kv_send.at[which, row],
            recv_sem=kv_recv.at[which, row],
            device_id=(other, row),
            device_id_type=MESH,
        ).wait_recv()

    len_copy = pltpu.make_async_remote_copy(
        src_ref=lens_ref, dst_ref=len_in, send_sem=len_sem.at[0], recv_sem=len_sem.at[1],
        device_id=(other, tp), device_id_type=MESH,
    )
    len_copy.start()
    for k in range(n_tp):
        handoff(0, k).start()

    loads = [
        pltpu.make_async_copy(src, dst, load_sem.at[j])
        for j, (src, dst) in enumerate(
            (
                (query_ref, q_raw),
                (newkv_ref, nk_raw),
                (lens_ref, len_raw),
                (resident_ref, resident),
                (resid_ref, rs_raw),
                (weight_ref, weight),
            )
        )
    ]
    for load in loads:
        load.start()
    for load in loads[:3]:
        load.wait()
    qf[...] = q_raw[0].astype(F32)
    nkf[...] = nk_raw[0, :, :, pl.ds(column(tp), wide)].astype(F32)

    head = lax.broadcasted_iota(jnp.int32, (per_dev, HD), 0)
    place = lax.broadcasted_iota(jnp.int32, (per_dev, span), 1)

    def probabilities(row, keys, length):
        q = jnp.concatenate([qf[row : row + 1, h * HD : (h + 1) * HD] for h in range(per_dev)], axis=0)
        spread = jnp.concatenate(
            [jnp.where(head // per_kv == s, q, 0.0) for s in range(kv_dev)], axis=1
        )
        score = lax.dot_general(
            spread.astype(BF16), keys, (((1,), (1,)), ((), ())), preferred_element_type=F32
        ) * scale
        own = jnp.sum(spread * nkf[row, 0:1, :], axis=1, keepdims=True) * scale
        live = place < length
        score = jnp.where(live, score, -1e30)
        top = jnp.maximum(jnp.max(score, axis=1, keepdims=True), own)
        part = jnp.where(live, jnp.exp(score - top), 0.0)
        own_part = jnp.exp(own - top)
        total = jnp.sum(part, axis=1, keepdims=True) + own_part
        return (part / total).astype(BF16), (own_part / total).astype(BF16).astype(F32)

    def blend(row, out, out_row, p, own_p, values):
        o = jnp.dot(p, values, preferred_element_type=F32) + own_p * nkf[row, 1:2, :]
        for h in range(per_dev):
            s = h // per_kv
            out[out_row : out_row + 1, h * HD : (h + 1) * HD] = o[h : h + 1, s * HD : (s + 1) * HD]

    def length_of(lens, row):
        lane = lax.broadcasted_iota(jnp.int32, lens.shape, 1)
        return jnp.sum(jnp.where(lane == row, lens, 0), axis=1, keepdims=True)

    loads[3].wait()

    for r in range(res_rows):
        row = adopt + r
        p, own_p = probabilities(row, resident[0, 0, r, 0], length_of(len_raw[...], row))
        blend(row, attn_a, r, p, own_p, resident[0, 0, r, 1])

    loads[4].wait()
    resf[...] = rs_raw[0].astype(F32)
    loads[5].wait()

    def project(attn, rows, rank, first_row, with_residual):
        pieces = max(1, TILE // rows)
        width = share // pieces
        a = attn[0:rows, :].astype(BF16)
        parts = []
        for j in range(pieces):
            at = pl.multiple_of(rank * share + j * width, HD)
            value = jnp.dot(a, weight[:, pl.ds(at, width)], preferred_element_type=F32)
            if with_residual:
                value = value + resf[first_row : first_row + rows, pl.ds(at, width)]
            parts.append(value)
        return jnp.concatenate(parts, axis=0)

    def push(src, dst, send, recv, rank, o):
        return pltpu.make_async_remote_copy(
            src_ref=src, dst_ref=dst, send_sem=send.at[o], recv_sem=recv.at[tp],
            device_id=(inst, rank), device_id_type=MESH,
        )

    def landed(buf, send, recv, rank):
        pltpu.make_async_remote_copy(
            src_ref=buf.at[rank], dst_ref=buf.at[rank], send_sem=send.at[0], recv_sem=recv.at[rank],
            device_id=(inst, rank), device_id_type=MESH,
        ).wait_recv()

    def scatter(attn, rows, first_row, buf, land, total, send, recv):
        @pl.loop(1, n_tp)
        def _(o):
            rank = lax.rem(tp + o, n_tp)
            buf[o] = project(attn, rows, rank, first_row, False).astype(BF16)
            push(buf.at[o], land.at[tp], send, recv, rank, o).start()

        total[...] = project(attn, rows, tp, first_row, True)

    def gather(buf, land, everything, total, rs_send, rs_recv, send, recv):
        for o in range(1, n_tp):
            rank = lax.rem(tp + o, n_tp)
            landed(land, rs_send, rs_recv, rank)
            total[...] += land[rank].astype(F32)
        everything[tp] = total[...].astype(BF16)
        for o in range(1, n_tp):
            push(everything.at[tp], everything.at[tp], send, recv, lax.rem(tp + o, n_tp), o).start()
        for o in range(1, n_tp):
            push(buf.at[o], land.at[tp], rs_send, rs_recv, lax.rem(tp + o, n_tp), o).wait_send()

    def finish(everything, rows, first_row, send, recv):
        for o in range(1, n_tp):
            landed(everything, send, recv, lax.rem(tp + o, n_tp))
        pieces = max(1, TILE // rows)
        width = share // pieces
        for rank in range(n_tp):
            block = everything[rank].astype(F32)
            for j in range(pieces):
                at = rank * share + j * width
                mixed_ref[first_row : first_row + rows, at : at + width] = block[j * rows : (j + 1) * rows]
        for o in range(1, n_tp):
            push(everything.at[tp], everything.at[tp], send, recv, lax.rem(tp + o, n_tp), o).wait_send()

    def keep(which, row):
        return pltpu.make_async_copy(
            cache.at[row, which], adopted_ref.at[0, 0, row, which], out_sem.at[which, row]
        )

    scatter(attn_a, res_rows, adopt, send_a, land_a, total_a, rs_send_a, rs_recv_a)
    for k in range(n_tp):
        handoff(0, k).wait_send()
        handoff(1, k).start()
    gather(send_a, land_a, all_a, total_a, rs_send_a, rs_recv_a, ag_send_a, ag_recv_a)

    len_copy.wait_recv()
    for row in range(adopt):
        arrived(0, row)
        keep(0, row).start()
        p, own_p = probabilities(row, cache[row, 0], len_in[:, row : row + 1])
        prob[row] = p.astype(F32)
        own_prob[row] = jnp.broadcast_to(own_p, (per_dev, HD))
    finish(all_a, res_rows, adopt, ag_send_a, ag_recv_a)

    for row in range(adopt):
        arrived(1, row)
        keep(1, row).start()
        blend(row, attn_b, row, prob[row].astype(BF16), own_prob[row][:, 0:1], cache[row, 1])
    scatter(attn_b, adopt, 0, send_b, land_b, total_b, rs_send_b, rs_recv_b)
    gather(send_b, land_b, all_b, total_b, rs_send_b, rs_recv_b, ag_send_b, ag_recv_b)
    finish(all_b, adopt, 0, ag_send_b, ag_recv_b)

    len_copy.wait_send()
    for k in range(n_tp):
        handoff(1, k).wait_send()
    for which in range(2):
        for row in range(adopt):
            keep(which, row).wait()


def on_device(n_inst, n_tp, source_cache, resident_cache, new_kv, queries, residual, lengths, out_weight):
    rows = queries.shape[1]
    span = source_cache.shape[3]
    adopt = source_cache.shape[1] * n_tp
    res_rows = resident_cache.shape[2]
    per_dev = queries.shape[2] // HD
    group = QH // KVH
    kv_dev = max(1, per_dev // group)
    per_kv = per_dev // kv_dev
    wide = kv_dev * HD
    depth, model = out_weight.shape
    share = model // n_tp
    fold_a = (TILE if res_rows < TILE else res_rows, share // max(1, TILE // res_rows))
    fold_b = (TILE if adopt < TILE else adopt, share // max(1, TILE // adopt))
    dims = (n_inst, n_tp, adopt, res_rows, kv_dev, per_kv, span)
    dma = pltpu.SemaphoreType.DMA
    any_spec = pl.BlockSpec(memory_space=pl.ANY)
    mixed, adopted = pl.pallas_call(
        functools.partial(kernel, dims),
        out_shape=(
            jax.ShapeDtypeStruct((rows, model), F32),
            jax.ShapeDtypeStruct((1, 1, adopt, 2, span, wide), BF16),
        ),
        in_specs=[any_spec] * 7,
        out_specs=(pl.BlockSpec(memory_space=pltpu.VMEM), any_spec),
        scratch_shapes=[
            pltpu.VMEM((adopt, 2, span, wide), BF16),
            pltpu.VMEM(resident_cache.shape, BF16),
            pltpu.VMEM(out_weight.shape, BF16),
            pltpu.VMEM(queries.shape, BF16),
            pltpu.VMEM(new_kv.shape, BF16),
            pltpu.VMEM(residual.shape, BF16),
            pltpu.VMEM(lengths.shape, jnp.int32),
            pltpu.VMEM(lengths.shape, jnp.int32),
            pltpu.VMEM(queries.shape[1:], F32),
            pltpu.VMEM((rows, 2, wide), F32),
            pltpu.VMEM((rows, model), F32),
            pltpu.VMEM((res_rows, depth), F32),
            pltpu.VMEM((adopt, depth), F32),
            pltpu.VMEM((adopt, per_dev, span), F32),
            pltpu.VMEM((adopt, per_dev, HD), F32),
            pltpu.VMEM((n_tp,) + fold_a, BF16),
            pltpu.VMEM((n_tp,) + fold_a, BF16),
            pltpu.VMEM((n_tp,) + fold_a, BF16),
            pltpu.VMEM((n_tp,) + fold_b, BF16),
            pltpu.VMEM((n_tp,) + fold_b, BF16),
            pltpu.VMEM((n_tp,) + fold_b, BF16),
            pltpu.VMEM(fold_a, F32),
            pltpu.VMEM(fold_b, F32),
            dma((2, n_tp)),
            dma((2, n_tp)),
            dma((2,)),
            dma((6,)),
            dma((2, adopt)),
        ]
        + [dma((n_tp,))] * 8,
        compiler_params=pltpu.CompilerParams(
            collective_id=0, has_side_effects=True, vmem_limit_bytes=48 * 1024 * 1024
        ),
        cost_estimate=pl.CostEstimate(
            flops=2 * rows * depth * model, bytes_accessed=2 * depth * model, transcendentals=0
        ),
        name="handoff_attention",
    )(source_cache, resident_cache, new_kv, queries, residual, lengths, out_weight)
    return (mixed.astype(BF16)[None], adopted)


def solution(mesh):
    in_specs = (
        P("inst", "tp", None, None, None),
        P("inst", "tp", None, None, None, None),
        P("inst", None, None, None),
        P("inst", None, "tp"),
        P("inst", None, None),
        P("inst", None),
        P("tp", None),
    )
    out_specs = (P("inst", None, None), P("inst", "tp", None, None, None, None))
    return jax.shard_map(
        functools.partial(on_device, mesh.shape["inst"], mesh.shape["tp"]),
        mesh=mesh, in_specs=in_specs, out_specs=out_specs, check_vma=False,
    )
```

```python
import functools
import math

import jax
import jax.numpy as jnp
from jax import lax
from jax.experimental import pallas as pl
from jax.experimental.pallas import tpu as pltpu
from jax.sharding import PartitionSpec as P

HD = 128
KVH = 8
QH = 32
TILE = 16
MESH = pl.DeviceIdType.MESH
BF16 = jnp.bfloat16
F32 = jnp.float32


def pieces_of(rows):
    return TILE // math.gcd(rows, TILE)


def kernel(
    dims,
    source_ref, resident_ref, newkv_ref, query_ref, resid_ref, lens_ref, weight_ref,
    mixed_ref, adopted_ref,
    source, resident, weight, q_raw, nk_raw, rs_raw, len_raw,
    qf, q_rows, q_in, nkf, nk_out, nk_in, resf, o_out, o_in, attn,
    part_out, part_in, final, total, mixed,
    kv_send, kv_recv, load_sem, q_send, q_recv, nk_sem, o_send, o_recv,
    rs_send, rs_recv, ag_send, ag_recv,
):
    n_inst, n_tp, adopt, res_rows, kv_dev, per_kv, span = dims
    rows = adopt + res_rows
    per_dev = kv_dev * per_kv
    group = QH // KVH
    wide = kv_dev * HD
    inst, tp = lax.axis_index("inst"), lax.axis_index("tp")
    other = lax.rem(inst + n_inst // 2, n_inst)
    scale = 1.0 / math.sqrt(HD)
    model = weight_ref.shape[1]
    share = model // n_tp
    pieces = pieces_of(rows)
    width = share // pieces

    def column(rank):
        return rank * per_dev // group * HD

    def my_columns(rank):
        return pl.ds(pl.multiple_of(column(rank), HD), wide)

    barrier = pltpu.get_barrier_semaphore()
    for o in range(n_tp):
        pl.semaphore_signal(barrier, inc=1, device_id=(other, lax.rem(tp + o, n_tp)), device_id_type=MESH)
        if o > 0:
            pl.semaphore_signal(barrier, inc=1, device_id=(inst, lax.rem(tp + o, n_tp)), device_id_type=MESH)
    loads = [
        pltpu.make_async_copy(src, dst, load_sem.at[j])
        for j, (src, dst) in enumerate(
            (
                (query_ref, q_raw),
                (newkv_ref, nk_raw),
                (lens_ref, len_raw),
                (resident_ref, resident),
                (source_ref, source),
                (resid_ref, rs_raw),
                (weight_ref, weight),
            )
        )
    ]
    for load in loads[:3]:
        load.start()
    pl.semaphore_wait(barrier, 2 * n_tp - 1)

    core = lax.rem(inst, 2)

    def handoff(which, k):
        base = (k // 2 + (n_tp // 2 if k % 2 == 0 else 0)) % n_tp
        rank = lax.rem(tp + base + core * (n_tp // 2), n_tp)
        return pltpu.make_async_remote_copy(
            src_ref=source_ref.at[0, 0, which, :, my_columns(rank)],
            dst_ref=adopted_ref.at[0, 0, tp, which],
            send_sem=kv_send.at[which, k],
            recv_sem=kv_recv.at[which, tp],
            device_id=(other, rank),
            device_id_type=MESH,
        )

    def send(src, dst, send_sem, recv_sem, device):
        return pltpu.make_async_remote_copy(
            src_ref=src, dst_ref=dst, send_sem=send_sem, recv_sem=recv_sem,
            device_id=device, device_id_type=MESH,
        )

    for k in range(n_tp):
        handoff(0, k).start()
    for load in loads[3:]:
        load.start()
    for load in loads[:3]:
        load.wait()

    def rows_to_heads(first, last):
        for row in range(first, last):
            q_rows[row] = jnp.concatenate(
                [qf[row : row + 1, h * HD : (h + 1) * HD] for h in range(per_dev)], axis=0
            )

    qf[...] = q_raw[0].astype(F32)
    nk_out[...] = nk_raw[0, tp].astype(F32)
    rows_to_heads(0, adopt)
    q_sends = [
        send(q_rows.at[r], q_in.at[tp], q_send.at[r], q_recv.at[tp], (other, r)) for r in range(adopt)
    ]
    nk_send = send(nk_out, nk_in, nk_sem.at[0], nk_sem.at[1], (other, tp))
    for copy in q_sends:
        copy.start()
    nk_send.start()
    rows_to_heads(adopt, rows)
    nkf[...] = nk_raw[0, :, :, my_columns(tp)].astype(F32)

    head = lax.broadcasted_iota(jnp.int32, (per_dev, HD), 0)
    place = lax.broadcasted_iota(jnp.int32, (per_dev, span), 1)

    def attention(q, keys, values, own_key, own_value, length):
        spread = jnp.concatenate(
            [jnp.where(head // per_kv == s, q, 0.0) for s in range(kv_dev)], axis=1
        )
        score = lax.dot_general(
            spread.astype(BF16), keys, (((1,), (1,)), ((), ())), preferred_element_type=F32
        ) * scale
        own = jnp.sum(spread * own_key, axis=1, keepdims=True) * scale
        live = place < length
        score = jnp.where(live, score, -1e30)
        top = jnp.maximum(jnp.max(score, axis=1, keepdims=True), own)
        part = jnp.where(live, jnp.exp(score - top), 0.0)
        own_part = jnp.exp(own - top)
        whole = jnp.sum(part, axis=1, keepdims=True) + own_part
        p = (part / whole).astype(BF16)
        own_p = (own_part / whole).astype(BF16).astype(F32)
        o = jnp.dot(p, values, preferred_element_type=F32) + own_p * own_value
        result = o[:, 0:HD]
        for s in range(1, kv_dev):
            result = jnp.where(head // per_kv == s, o[:, s * HD : (s + 1) * HD], result)
        return result

    def place_row(row, heads):
        for h in range(per_dev):
            attn[row : row + 1, h * HD : (h + 1) * HD] = heads[h : h + 1, :]

    lens = len_raw[...]
    lane = lax.broadcasted_iota(jnp.int32, lens.shape, 1)
    handed = jnp.sum(jnp.where(lane == tp, lens, 0), axis=1, keepdims=True)

    def serve(row):
        r = row - adopt
        place_row(
            row,
            attention(
                q_rows[row], resident[0, 0, r, 0], resident[0, 0, r, 1],
                nkf[row, 0:1, :], nkf[row, 1:2, :], lens[:, row : row + 1],
            ),
        )

    loads[3].wait()
    for row in range(adopt, adopt + res_rows // 2):
        serve(row)

    loads[4].wait()
    nk_send.wait_recv()
    for rank in range(n_tp):
        send(q_rows.at[rank], q_in.at[rank], q_send.at[rank], q_recv.at[rank], (other, rank)).wait_recv()
    o_sends = []
    for rank in range(n_tp):
        at = column(rank)
        o_out[rank] = attention(
            q_in[rank], source[0, 0, 0, :, at : at + wide], source[0, 0, 1, :, at : at + wide],
            nk_in[0:1, at : at + wide], nk_in[1:2, at : at + wide], handed,
        )
        copy = send(o_out.at[rank], o_in.at[tp], o_send.at[rank], o_recv.at[tp], (other, rank))
        copy.start()
        o_sends.append(copy)
    for k in range(n_tp // 2):
        handoff(1, k).start()

    for row in range(adopt + res_rows // 2, rows):
        serve(row)
    loads[5].wait()
    resf[...] = rs_raw[0].astype(F32)
    for row in range(adopt):
        send(o_out.at[row], o_in.at[row], o_send.at[row], o_recv.at[row], (other, row)).wait_recv()
        place_row(row, o_in[row])
    loads[6].wait()

    def project(rank, with_residual):
        a = attn[...].astype(BF16)
        parts = []
        for j in range(pieces):
            at = pl.multiple_of(rank * share + j * width, HD)
            value = jnp.dot(a, weight[:, pl.ds(at, width)], preferred_element_type=F32)
            if with_residual:
                value = value + resf[:, pl.ds(at, width)]
            parts.append(value)
        return jnp.concatenate(parts, axis=0)

    @pl.loop(1, n_tp)
    def _(o):
        rank = lax.rem(tp + o, n_tp)
        part_out[o] = project(rank, False).astype(BF16)
        send(part_out.at[o], part_in.at[tp], rs_send.at[o], rs_recv.at[tp], (inst, rank)).start()

    for k in range(n_tp // 2, n_tp):
        handoff(1, k).start()
    total[...] = project(tp, True)
    for o in range(1, n_tp):
        rank = lax.rem(tp + o, n_tp)
        send(part_out.at[o], part_in.at[rank], rs_send.at[o], rs_recv.at[rank], (inst, rank)).wait_recv()
        total[...] += part_in[rank].astype(F32)
    final[tp] = total[...].astype(BF16)

    def give(o):
        rank = lax.rem(tp + o, n_tp)
        return send(final.at[tp], final.at[tp], ag_send.at[o], ag_recv.at[tp], (inst, rank))

    for o in range(1, n_tp):
        give(o).start()
    for o in range(1, n_tp):
        rank = lax.rem(tp + o, n_tp)
        send(final.at[rank], final.at[rank], ag_send.at[o], ag_recv.at[rank], (inst, rank)).wait_recv()
    for rank in range(n_tp):
        block = final[rank].astype(F32)
        for j in range(pieces):
            at = rank * share + j * width
            mixed[:, at : at + width] = block[j * rows : (j + 1) * rows].astype(BF16)
    mixed_copy = pltpu.make_async_copy(mixed, mixed_ref, load_sem.at[7])
    mixed_copy.start()

    mixed_copy.wait()
    for copy in q_sends:
        copy.wait_send()
    nk_send.wait_send()
    for copy in o_sends:
        copy.wait_send()
    for o in range(1, n_tp):
        rank = lax.rem(tp + o, n_tp)
        send(part_out.at[o], part_in.at[tp], rs_send.at[o], rs_recv.at[tp], (inst, rank)).wait_send()
        give(o).wait_send()
    for which in range(2):
        for k in range(n_tp):
            handoff(which, k).wait_send()
            there = adopted_ref.at[0, 0, k, which]
            send(there, there, kv_send.at[which, k], kv_recv.at[which, k], (other, k)).wait_recv()


def on_device(n_inst, n_tp, source_cache, resident_cache, new_kv, queries, residual, lengths, out_weight):
    rows = queries.shape[1]
    span = source_cache.shape[3]
    adopt = source_cache.shape[1] * n_tp
    res_rows = resident_cache.shape[2]
    per_dev = queries.shape[2] // HD
    group = QH // KVH
    kv_dev = max(1, per_dev // group)
    per_kv = per_dev // kv_dev
    wide = kv_dev * HD
    depth, model = out_weight.shape
    pieces = pieces_of(rows)
    stack = (rows * pieces, model // n_tp // pieces)
    dims = (n_inst, n_tp, adopt, res_rows, kv_dev, per_kv, span)
    dma = pltpu.SemaphoreType.DMA
    any_spec = pl.BlockSpec(memory_space=pl.ANY)
    mixed, adopted = pl.pallas_call(
        functools.partial(kernel, dims),
        out_shape=(
            jax.ShapeDtypeStruct((rows, model), BF16),
            jax.ShapeDtypeStruct((1, 1, adopt, 2, span, wide), BF16),
        ),
        in_specs=[pl.BlockSpec(memory_space=pltpu.HBM)] * 7,
        out_specs=(any_spec, any_spec),
        scratch_shapes=[
            pltpu.VMEM(source_cache.shape, BF16),
            pltpu.VMEM(resident_cache.shape, BF16),
            pltpu.VMEM(out_weight.shape, BF16),
            pltpu.VMEM(queries.shape, BF16),
            pltpu.VMEM(new_kv.shape, BF16),
            pltpu.VMEM(residual.shape, BF16),
            pltpu.VMEM(lengths.shape, jnp.int32),
            pltpu.VMEM(queries.shape[1:], F32),
            pltpu.VMEM((rows, per_dev, HD), F32),
            pltpu.VMEM((n_tp, per_dev, HD), F32),
            pltpu.VMEM((rows, 2, wide), F32),
            pltpu.VMEM(new_kv.shape[2:], F32),
            pltpu.VMEM(new_kv.shape[2:], F32),
            pltpu.VMEM((rows, model), F32),
            pltpu.VMEM((n_tp, per_dev, HD), F32),
            pltpu.VMEM((adopt, per_dev, HD), F32),
            pltpu.VMEM((rows, depth), F32),
            pltpu.VMEM((n_tp,) + stack, BF16),
            pltpu.VMEM((n_tp,) + stack, BF16),
            pltpu.VMEM((n_tp,) + stack, BF16),
            pltpu.VMEM(stack, F32),
            pltpu.VMEM((rows, model), BF16),
            dma((2, n_tp)),
            dma((2, n_tp)),
            dma((8,)),
            dma((adopt,)),
            dma((n_tp,)),
            dma((2,)),
            dma((n_tp,)),
            dma((adopt,)),
        ]
        + [dma((n_tp,))] * 4,
        compiler_params=pltpu.CompilerParams(
            collective_id=0, has_side_effects=True, vmem_limit_bytes=60 * 1024 * 1024
        ),
        cost_estimate=pl.CostEstimate(
            flops=2 * rows * depth * model, bytes_accessed=2 * depth * model, transcendentals=0
        ),
        name="handoff_attention",
    )(source_cache, resident_cache, new_kv, queries, residual, lengths, out_weight)
    return (mixed[None], adopted)


def solution(mesh):
    in_specs = (
        P("inst", "tp", None, None, None),
        P("inst", "tp", None, None, None, None),
        P("inst", None, None, None),
        P("inst", None, "tp"),
        P("inst", None, None),
        P("inst", None),
        P("tp", None),
    )
    out_specs = (P("inst", None, None), P("inst", "tp", None, None, None, None))
    return jax.shard_map(
        functools.partial(on_device, mesh.shape["inst"], mesh.shape["tp"]),
        mesh=mesh, in_specs=in_specs, out_specs=out_specs, check_vma=False,
    )
```

```python
import functools
import math

import jax
import jax.numpy as jnp
from jax import lax
from jax.experimental import pallas as pl
from jax.experimental.pallas import tpu as pltpu
from jax.sharding import PartitionSpec as P

HD = 128
KVH = 8
QH = 32
TILE = 16
MESH = pl.DeviceIdType.MESH
BF16 = jnp.bfloat16
F32 = jnp.float32


def pieces_of(rows):
    return TILE // math.gcd(rows, TILE)


def kernel(
    dims,
    source_ref, resident_ref, newkv_ref, query_ref, resid_ref, lens_ref, weight_ref,
    mixed_ref, adopted_ref,
    source, resident, weight, q_raw, nk_raw, rs_raw, len_raw,
    qf, q_rows, q_in, nkf, nk_out, nk_in, resf, o_out, o_in, attn,
    part_out, part_in, final, total, mixed,
    kv_send, kv_recv, load_sem, q_send, q_recv, nk_sem, o_send, o_recv,
    rs_send, rs_recv, ag_send, ag_recv,
):
    n_inst, n_tp, adopt, res_rows, kv_dev, per_kv, span = dims
    rows = adopt + res_rows
    per_dev = kv_dev * per_kv
    group = QH // KVH
    wide = kv_dev * HD
    inst, tp = lax.axis_index("inst"), lax.axis_index("tp")
    other = lax.rem(inst + n_inst // 2, n_inst)
    scale = 1.0 / math.sqrt(HD)
    model = weight_ref.shape[1]
    share = model // n_tp
    pieces = pieces_of(rows)
    width = share // pieces

    def column(rank):
        return rank * per_dev // group * HD

    def my_columns(rank):
        return pl.ds(pl.multiple_of(column(rank), HD), wide)

    barrier = pltpu.get_barrier_semaphore()
    for o in range(n_tp):
        pl.semaphore_signal(barrier, inc=1, device_id=(other, lax.rem(tp + o, n_tp)), device_id_type=MESH)
        if o > 0:
            pl.semaphore_signal(barrier, inc=1, device_id=(inst, lax.rem(tp + o, n_tp)), device_id_type=MESH)
    loads = [
        pltpu.make_async_copy(src, dst, load_sem.at[j])
        for j, (src, dst) in enumerate(
            (
                (query_ref, q_raw),
                (newkv_ref, nk_raw),
                (lens_ref, len_raw),
                (resident_ref, resident),
                (source_ref, source),
                (resid_ref, rs_raw),
                (weight_ref, weight),
            )
        )
    ]
    for load in loads[:3]:
        load.start()
    pl.semaphore_wait(barrier, 2 * n_tp - 1)

    core = lax.rem(inst, 2)

    half = span // 2

    def handoff(j):
        phase, k = j // n_tp, j % n_tp
        which, piece = phase // 2, phase % 2
        base = (k // 2 + (n_tp // 2 if k % 2 == 0 else 0)) % n_tp
        rank = lax.rem(tp + base + core * (n_tp // 2), n_tp)
        rows_of = pl.ds(piece * half, half)
        return pltpu.make_async_remote_copy(
            src_ref=source_ref.at[0, 0, which, rows_of, my_columns(rank)],
            dst_ref=adopted_ref.at[0, 0, tp, which, rows_of],
            send_sem=kv_send.at[phase, k],
            recv_sem=kv_recv.at[phase, tp],
            device_id=(other, rank),
            device_id_type=MESH,
        )

    def start_handoff(first, last):
        for j in range(first * n_tp // 4, last * n_tp // 4):
            handoff(j).start()

    def send(src, dst, send_sem, recv_sem, device):
        return pltpu.make_async_remote_copy(
            src_ref=src, dst_ref=dst, send_sem=send_sem, recv_sem=recv_sem,
            device_id=device, device_id_type=MESH,
        )

    start_handoff(0, 2)
    for load in loads[3:]:
        load.start()
    for load in loads[:3]:
        load.wait()

    def rows_to_heads(first, last):
        for row in range(first, last):
            q_rows[row] = jnp.concatenate(
                [qf[row : row + 1, h * HD : (h + 1) * HD] for h in range(per_dev)], axis=0
            )

    qf[...] = q_raw[0].astype(F32)
    nk_out[...] = nk_raw[0, tp].astype(F32)
    rows_to_heads(0, adopt)
    q_sends = [
        send(q_rows.at[r], q_in.at[tp], q_send.at[r], q_recv.at[tp], (other, r)) for r in range(adopt)
    ]
    nk_send = send(nk_out, nk_in, nk_sem.at[0], nk_sem.at[1], (other, tp))
    for copy in q_sends:
        copy.start()
    nk_send.start()
    start_handoff(2, 6)
    rows_to_heads(adopt, rows)
    nkf[...] = nk_raw[0, :, :, my_columns(tp)].astype(F32)

    head = lax.broadcasted_iota(jnp.int32, (per_dev, HD), 0)
    place = lax.broadcasted_iota(jnp.int32, (per_dev, span), 1)

    def attention(q, keys, values, own_key, own_value, length):
        spread = jnp.concatenate(
            [jnp.where(head // per_kv == s, q, 0.0) for s in range(kv_dev)], axis=1
        )
        score = lax.dot_general(
            spread.astype(BF16), keys, (((1,), (1,)), ((), ())), preferred_element_type=F32
        ) * scale
        own = jnp.sum(spread * own_key, axis=1, keepdims=True) * scale
        live = place < length
        score = jnp.where(live, score, -1e30)
        top = jnp.maximum(jnp.max(score, axis=1, keepdims=True), own)
        part = jnp.where(live, jnp.exp(score - top), 0.0)
        own_part = jnp.exp(own - top)
        whole = jnp.sum(part, axis=1, keepdims=True) + own_part
        p = (part / whole).astype(BF16)
        own_p = (own_part / whole).astype(BF16).astype(F32)
        o = jnp.dot(p, values, preferred_element_type=F32) + own_p * own_value
        result = o[:, 0:HD]
        for s in range(1, kv_dev):
            result = jnp.where(head // per_kv == s, o[:, s * HD : (s + 1) * HD], result)
        return result

    def place_row(row, heads):
        for h in range(per_dev):
            attn[row : row + 1, h * HD : (h + 1) * HD] = heads[h : h + 1, :]

    lens = len_raw[...]
    lane = lax.broadcasted_iota(jnp.int32, lens.shape, 1)
    handed = jnp.sum(jnp.where(lane == tp, lens, 0), axis=1, keepdims=True)

    def serve(row):
        r = row - adopt
        place_row(
            row,
            attention(
                q_rows[row], resident[0, 0, r, 0], resident[0, 0, r, 1],
                nkf[row, 0:1, :], nkf[row, 1:2, :], lens[:, row : row + 1],
            ),
        )

    loads[3].wait()
    for row in range(adopt, adopt + res_rows // 2):
        serve(row)

    loads[4].wait()
    nk_send.wait_recv()
    for rank in range(n_tp):
        send(q_rows.at[rank], q_in.at[rank], q_send.at[rank], q_recv.at[rank], (other, rank)).wait_recv()
    o_sends = []
    for rank in range(n_tp):
        at = column(rank)
        o_out[rank] = attention(
            q_in[rank], source[0, 0, 0, :, at : at + wide], source[0, 0, 1, :, at : at + wide],
            nk_in[0:1, at : at + wide], nk_in[1:2, at : at + wide], handed,
        )
        copy = send(o_out.at[rank], o_in.at[tp], o_send.at[rank], o_recv.at[tp], (other, rank))
        copy.start()
        o_sends.append(copy)
    start_handoff(6, 10)

    for row in range(adopt + res_rows // 2, rows):
        serve(row)
    loads[5].wait()
    resf[...] = rs_raw[0].astype(F32)
    for row in range(adopt):
        send(o_out.at[row], o_in.at[row], o_send.at[row], o_recv.at[row], (other, row)).wait_recv()
        place_row(row, o_in[row])
    loads[6].wait()

    def project(rank, with_residual):
        a = attn[...].astype(BF16)
        parts = []
        for j in range(pieces):
            at = pl.multiple_of(rank * share + j * width, HD)
            value = jnp.dot(a, weight[:, pl.ds(at, width)], preferred_element_type=F32)
            if with_residual:
                value = value + resf[:, pl.ds(at, width)]
            parts.append(value)
        return jnp.concatenate(parts, axis=0)

    @pl.loop(1, n_tp)
    def _(o):
        rank = lax.rem(tp + o, n_tp)
        part_out[o] = project(rank, False).astype(BF16)
        send(part_out.at[o], part_in.at[tp], rs_send.at[o], rs_recv.at[tp], (inst, rank)).start()

    start_handoff(10, 12)
    total[...] = project(tp, True)
    for o in range(1, n_tp):
        rank = lax.rem(tp + o, n_tp)
        send(part_out.at[o], part_in.at[rank], rs_send.at[o], rs_recv.at[rank], (inst, rank)).wait_recv()
        total[...] += part_in[rank].astype(F32)
    final[tp] = total[...].astype(BF16)

    def give(o):
        rank = lax.rem(tp + o, n_tp)
        return send(final.at[tp], final.at[tp], ag_send.at[o], ag_recv.at[tp], (inst, rank))

    for o in range(1, n_tp):
        give(o).start()
    start_handoff(12, 16)
    for o in range(1, n_tp):
        rank = lax.rem(tp + o, n_tp)
        send(final.at[rank], final.at[rank], ag_send.at[o], ag_recv.at[rank], (inst, rank)).wait_recv()
    for rank in range(n_tp):
        block = final[rank].astype(F32)
        for j in range(pieces):
            at = rank * share + j * width
            mixed[:, at : at + width] = block[j * rows : (j + 1) * rows].astype(BF16)
    mixed_copy = pltpu.make_async_copy(mixed, mixed_ref, load_sem.at[7])
    mixed_copy.start()

    mixed_copy.wait()
    for copy in q_sends:
        copy.wait_send()
    nk_send.wait_send()
    for copy in o_sends:
        copy.wait_send()
    for o in range(1, n_tp):
        rank = lax.rem(tp + o, n_tp)
        send(part_out.at[o], part_in.at[tp], rs_send.at[o], rs_recv.at[tp], (inst, rank)).wait_send()
        give(o).wait_send()
    for j in range(4 * n_tp):
        handoff(j).wait_send()
        phase, k = j // n_tp, j % n_tp
        there = adopted_ref.at[0, 0, k, phase // 2, pl.ds(phase % 2 * half, half)]
        send(there, there, kv_send.at[phase, k], kv_recv.at[phase, k], (other, k)).wait_recv()


def place_outputs(mixed_ref, adopted_ref, mixed_out, adopted_out, sem):
    count = adopted_ref.shape[2]
    copies = [pltpu.make_async_copy(mixed_ref, mixed_out.at[0], sem.at[0])]
    for row in range(count):
        for which in range(2):
            copies.append(
                pltpu.make_async_copy(
                    adopted_ref.at[0, 0, row, which],
                    adopted_out.at[0, 0, row, which],
                    sem.at[1 + 2 * row + which],
                )
            )
    for copy in copies:
        copy.start()
    for copy in copies:
        copy.wait()


def on_device(n_inst, n_tp, source_cache, resident_cache, new_kv, queries, residual, lengths, out_weight):
    rows = queries.shape[1]
    span = source_cache.shape[3]
    adopt = source_cache.shape[1] * n_tp
    res_rows = resident_cache.shape[2]
    per_dev = queries.shape[2] // HD
    group = QH // KVH
    kv_dev = max(1, per_dev // group)
    per_kv = per_dev // kv_dev
    wide = kv_dev * HD
    depth, model = out_weight.shape
    pieces = pieces_of(rows)
    stack = (rows * pieces, model // n_tp // pieces)
    dims = (n_inst, n_tp, adopt, res_rows, kv_dev, per_kv, span)
    dma = pltpu.SemaphoreType.DMA
    any_spec = pl.BlockSpec(memory_space=pl.ANY)
    mixed, adopted = pl.pallas_call(
        functools.partial(kernel, dims),
        out_shape=(
            jax.ShapeDtypeStruct((rows, model), BF16),
            jax.ShapeDtypeStruct((1, 1, adopt, 2, span, wide), BF16),
        ),
        in_specs=[pl.BlockSpec(memory_space=pltpu.HBM)] * 7,
        out_specs=(any_spec, any_spec),
        scratch_shapes=[
            pltpu.VMEM(source_cache.shape, BF16),
            pltpu.VMEM(resident_cache.shape, BF16),
            pltpu.VMEM(out_weight.shape, BF16),
            pltpu.VMEM(queries.shape, BF16),
            pltpu.VMEM(new_kv.shape, BF16),
            pltpu.VMEM(residual.shape, BF16),
            pltpu.VMEM(lengths.shape, jnp.int32),
            pltpu.VMEM(queries.shape[1:], F32),
            pltpu.VMEM((rows, per_dev, HD), F32),
            pltpu.VMEM((n_tp, per_dev, HD), F32),
            pltpu.VMEM((rows, 2, wide), F32),
            pltpu.VMEM(new_kv.shape[2:], F32),
            pltpu.VMEM(new_kv.shape[2:], F32),
            pltpu.VMEM((rows, model), F32),
            pltpu.VMEM((n_tp, per_dev, HD), F32),
            pltpu.VMEM((adopt, per_dev, HD), F32),
            pltpu.VMEM((rows, depth), F32),
            pltpu.VMEM((n_tp,) + stack, BF16),
            pltpu.VMEM((n_tp,) + stack, BF16),
            pltpu.VMEM((n_tp,) + stack, BF16),
            pltpu.VMEM(stack, F32),
            pltpu.VMEM((rows, model), BF16),
            dma((4, n_tp)),
            dma((4, n_tp)),
            dma((8,)),
            dma((adopt,)),
            dma((n_tp,)),
            dma((2,)),
            dma((n_tp,)),
            dma((adopt,)),
        ]
        + [dma((n_tp,))] * 4,
        compiler_params=pltpu.CompilerParams(
            collective_id=0, has_side_effects=True, vmem_limit_bytes=60 * 1024 * 1024
        ),
        cost_estimate=pl.CostEstimate(
            flops=2 * rows * depth * model, bytes_accessed=2 * depth * model, transcendentals=0
        ),
        name="handoff_attention",
    )(source_cache, resident_cache, new_kv, queries, residual, lengths, out_weight)
    return pl.pallas_call(
        place_outputs,
        out_shape=(
            jax.ShapeDtypeStruct((1, rows, model), BF16),
            jax.ShapeDtypeStruct(adopted.shape, BF16),
        ),
        in_specs=[any_spec, any_spec],
        out_specs=(any_spec, any_spec),
        scratch_shapes=[dma((1 + 2 * adopt,))],
        compiler_params=pltpu.CompilerParams(vmem_limit_bytes=60 * 1024 * 1024),
        cost_estimate=pl.CostEstimate(flops=0, bytes_accessed=4 * adopted.size, transcendentals=0),
        name="place_outputs",
    )(mixed, adopted)


def solution(mesh):
    in_specs = (
        P("inst", "tp", None, None, None),
        P("inst", "tp", None, None, None, None),
        P("inst", None, None, None),
        P("inst", None, "tp"),
        P("inst", None, None),
        P("inst", None),
        P("tp", None),
    )
    out_specs = (P("inst", None, None), P("inst", "tp", None, None, None, None))
    return jax.shard_map(
        functools.partial(on_device, mesh.shape["inst"], mesh.shape["tp"]),
        mesh=mesh, in_specs=in_specs, out_specs=out_specs, check_vma=False,
    )
```

```python
import functools
import math

import jax
import jax.numpy as jnp
from jax import lax
from jax.experimental import pallas as pl
from jax.experimental.pallas import tpu as pltpu
from jax.sharding import PartitionSpec as P

HD = 128
KVH = 8
QH = 32
TILE = 16
MESH = pl.DeviceIdType.MESH
BF16 = jnp.bfloat16
F32 = jnp.float32


def pieces_of(rows):
    return TILE // math.gcd(rows, TILE)


def kernel(
    dims,
    source_ref, resident_ref, newkv_ref, query_ref, resid_ref, lens_ref, weight_ref,
    mixed_ref, adopted_ref,
    source, cache, resident, weight, q_raw, nk_raw, rs_raw, len_raw,
    qf, q_rows, q_in, nkf, nk_out, nk_in, resf, o_out, o_in, attn,
    part_out, part_in, final, total, mixed,
    kv_send, kv_recv, keep_sem, load_sem, q_send, q_recv, nk_sem, o_send, o_recv,
    rs_send, rs_recv, ag_send, ag_recv,
):
    n_inst, n_tp, adopt, res_rows, kv_dev, per_kv, span = dims
    rows = adopt + res_rows
    per_dev = kv_dev * per_kv
    group = QH // KVH
    wide = kv_dev * HD
    inst, tp = lax.axis_index("inst"), lax.axis_index("tp")
    other = lax.rem(inst + n_inst // 2, n_inst)
    scale = 1.0 / math.sqrt(HD)
    model = weight_ref.shape[1]
    share = model // n_tp
    pieces = pieces_of(rows)
    width = share // pieces

    def column(rank):
        return rank * per_dev // group * HD

    def my_columns(rank):
        return pl.ds(pl.multiple_of(column(rank), HD), wide)

    barrier = pltpu.get_barrier_semaphore()
    for o in range(n_tp):
        pl.semaphore_signal(barrier, inc=1, device_id=(other, lax.rem(tp + o, n_tp)), device_id_type=MESH)
        if o > 0:
            pl.semaphore_signal(barrier, inc=1, device_id=(inst, lax.rem(tp + o, n_tp)), device_id_type=MESH)
    loads = [
        pltpu.make_async_copy(src, dst, load_sem.at[j])
        for j, (src, dst) in enumerate(
            (
                (query_ref, q_raw),
                (newkv_ref, nk_raw),
                (lens_ref, len_raw),
                (source_ref, source),
                (resident_ref, resident),
                (resid_ref, rs_raw),
                (weight_ref, weight),
            )
        )
    ]
    for load in loads[:4]:
        load.start()
    pl.semaphore_wait(barrier, 2 * n_tp - 1)

    core = lax.rem(inst, 2)

    half = span // 2

    def handoff(j):
        phase, k = j // n_tp, j % n_tp
        which, piece = phase // 2, phase % 2
        base = (k // 2 + (n_tp // 2 if k % 2 == 0 else 0)) % n_tp
        rank = lax.rem(tp + base + core * (n_tp // 2), n_tp)
        rows_of = pl.ds(piece * half, half)
        return pltpu.make_async_remote_copy(
            src_ref=source.at[0, 0, which, rows_of, my_columns(rank)],
            dst_ref=cache.at[tp, which, rows_of],
            send_sem=kv_send.at[phase, k],
            recv_sem=kv_recv.at[phase, tp],
            device_id=(other, rank),
            device_id_type=MESH,
        )

    def keep(j):
        phase, k = j // n_tp, j % n_tp
        which, rows_of = phase // 2, pl.ds(phase % 2 * half, half)
        return pltpu.make_async_copy(
            cache.at[k, which, rows_of], adopted_ref.at[0, 0, k, which, rows_of], keep_sem.at[phase, k]
        )

    def start_handoff(first, last):
        for j in range(first * n_tp // 4, last * n_tp // 4):
            handoff(j).start()

    def send(src, dst, send_sem, recv_sem, device):
        return pltpu.make_async_remote_copy(
            src_ref=src, dst_ref=dst, send_sem=send_sem, recv_sem=recv_sem,
            device_id=device, device_id_type=MESH,
        )

    loads[3].wait()
    start_handoff(0, 2)
    for load in loads[4:]:
        load.start()
    for load in loads[:3]:
        load.wait()

    def rows_to_heads(first, last):
        for row in range(first, last):
            q_rows[row] = jnp.concatenate(
                [qf[row : row + 1, h * HD : (h + 1) * HD] for h in range(per_dev)], axis=0
            )

    qf[...] = q_raw[0].astype(F32)
    nk_out[...] = nk_raw[0, tp].astype(F32)
    rows_to_heads(0, adopt)
    q_sends = [
        send(q_rows.at[r], q_in.at[tp], q_send.at[r], q_recv.at[tp], (other, r)) for r in range(adopt)
    ]
    nk_send = send(nk_out, nk_in, nk_sem.at[0], nk_sem.at[1], (other, tp))
    for copy in q_sends:
        copy.start()
    nk_send.start()
    start_handoff(2, 6)
    rows_to_heads(adopt, rows)
    nkf[...] = nk_raw[0, :, :, my_columns(tp)].astype(F32)

    head = lax.broadcasted_iota(jnp.int32, (per_dev, HD), 0)
    place = lax.broadcasted_iota(jnp.int32, (per_dev, span), 1)

    def attention(q, keys, values, own_key, own_value, length):
        spread = jnp.concatenate(
            [jnp.where(head // per_kv == s, q, 0.0) for s in range(kv_dev)], axis=1
        )
        score = lax.dot_general(
            spread.astype(BF16), keys, (((1,), (1,)), ((), ())), preferred_element_type=F32
        ) * scale
        own = jnp.sum(spread * own_key, axis=1, keepdims=True) * scale
        live = place < length
        score = jnp.where(live, score, -1e30)
        top = jnp.maximum(jnp.max(score, axis=1, keepdims=True), own)
        part = jnp.where(live, jnp.exp(score - top), 0.0)
        own_part = jnp.exp(own - top)
        whole = jnp.sum(part, axis=1, keepdims=True) + own_part
        p = (part / whole).astype(BF16)
        own_p = (own_part / whole).astype(BF16).astype(F32)
        o = jnp.dot(p, values, preferred_element_type=F32) + own_p * own_value
        result = o[:, 0:HD]
        for s in range(1, kv_dev):
            result = jnp.where(head // per_kv == s, o[:, s * HD : (s + 1) * HD], result)
        return result

    def place_row(row, heads):
        for h in range(per_dev):
            attn[row : row + 1, h * HD : (h + 1) * HD] = heads[h : h + 1, :]

    lens = len_raw[...]
    lane = lax.broadcasted_iota(jnp.int32, lens.shape, 1)
    handed = jnp.sum(jnp.where(lane == tp, lens, 0), axis=1, keepdims=True)

    def serve(row):
        r = row - adopt
        place_row(
            row,
            attention(
                q_rows[row], resident[0, 0, r, 0], resident[0, 0, r, 1],
                nkf[row, 0:1, :], nkf[row, 1:2, :], lens[:, row : row + 1],
            ),
        )

    loads[4].wait()
    for row in range(adopt, adopt + res_rows // 2):
        serve(row)

    nk_send.wait_recv()
    for rank in range(n_tp):
        send(q_rows.at[rank], q_in.at[rank], q_send.at[rank], q_recv.at[rank], (other, rank)).wait_recv()
    o_sends = []
    for rank in range(n_tp):
        at = column(rank)
        o_out[rank] = attention(
            q_in[rank], source[0, 0, 0, :, at : at + wide], source[0, 0, 1, :, at : at + wide],
            nk_in[0:1, at : at + wide], nk_in[1:2, at : at + wide], handed,
        )
        copy = send(o_out.at[rank], o_in.at[tp], o_send.at[rank], o_recv.at[tp], (other, rank))
        copy.start()
        o_sends.append(copy)
    start_handoff(6, 10)

    for row in range(adopt + res_rows // 2, rows):
        serve(row)
    loads[5].wait()
    resf[...] = rs_raw[0].astype(F32)
    for row in range(adopt):
        send(o_out.at[row], o_in.at[row], o_send.at[row], o_recv.at[row], (other, row)).wait_recv()
        place_row(row, o_in[row])
    loads[6].wait()

    def project(rank, with_residual):
        a = attn[...].astype(BF16)
        parts = []
        for j in range(pieces):
            at = pl.multiple_of(rank * share + j * width, HD)
            value = jnp.dot(a, weight[:, pl.ds(at, width)], preferred_element_type=F32)
            if with_residual:
                value = value + resf[:, pl.ds(at, width)]
            parts.append(value)
        return jnp.concatenate(parts, axis=0)

    @pl.loop(1, n_tp)
    def _(o):
        rank = lax.rem(tp + o, n_tp)
        part_out[o] = project(rank, False).astype(BF16)
        send(part_out.at[o], part_in.at[tp], rs_send.at[o], rs_recv.at[tp], (inst, rank)).start()

    start_handoff(10, 12)
    total[...] = project(tp, True)
    for o in range(1, n_tp):
        rank = lax.rem(tp + o, n_tp)
        send(part_out.at[o], part_in.at[rank], rs_send.at[o], rs_recv.at[rank], (inst, rank)).wait_recv()
        total[...] += part_in[rank].astype(F32)
    final[tp] = total[...].astype(BF16)

    def give(o):
        rank = lax.rem(tp + o, n_tp)
        return send(final.at[tp], final.at[tp], ag_send.at[o], ag_recv.at[tp], (inst, rank))

    for o in range(1, n_tp):
        give(o).start()
    start_handoff(12, 16)
    for o in range(1, n_tp):
        rank = lax.rem(tp + o, n_tp)
        send(final.at[rank], final.at[rank], ag_send.at[o], ag_recv.at[rank], (inst, rank)).wait_recv()
    for rank in range(n_tp):
        block = final[rank].astype(F32)
        for j in range(pieces):
            at = rank * share + j * width
            mixed[:, at : at + width] = block[j * rows : (j + 1) * rows].astype(BF16)
    mixed_copy = pltpu.make_async_copy(mixed, mixed_ref, load_sem.at[7])
    mixed_copy.start()

    mixed_copy.wait()
    for copy in q_sends:
        copy.wait_send()
    nk_send.wait_send()
    for copy in o_sends:
        copy.wait_send()
    for o in range(1, n_tp):
        rank = lax.rem(tp + o, n_tp)
        send(part_out.at[o], part_in.at[tp], rs_send.at[o], rs_recv.at[tp], (inst, rank)).wait_send()
        give(o).wait_send()
    for j in range(4 * n_tp):
        handoff(j).wait_send()
        phase, k = j // n_tp, j % n_tp
        rows_of = pl.ds(phase % 2 * half, half)
        there = cache.at[k, phase // 2, rows_of]
        send(there, there, kv_send.at[phase, k], kv_recv.at[phase, k], (other, k)).wait_recv()
        keep(j).start()
    for j in range(4 * n_tp):
        keep(j).wait()


def place_outputs(mixed_ref, adopted_ref, mixed_out, adopted_out, mixed, cache, load_sem, store_sem):
    loads = [pltpu.make_async_copy(mixed_ref, mixed, load_sem.at[0])]
    stores = [pltpu.make_async_copy(mixed, mixed_out.at[0], store_sem.at[0])]
    for row in range(adopted_ref.shape[2]):
        for which in range(2):
            at = 1 + 2 * row + which
            there = cache.at[row, which]
            loads.append(pltpu.make_async_copy(adopted_ref.at[0, 0, row, which], there, load_sem.at[at]))
            stores.append(pltpu.make_async_copy(there, adopted_out.at[0, 0, row, which], store_sem.at[at]))
    for load in loads:
        load.start()
    for load, store in zip(loads, stores):
        load.wait()
        store.start()
    for store in stores:
        store.wait()


def on_device(n_inst, n_tp, source_cache, resident_cache, new_kv, queries, residual, lengths, out_weight):
    rows = queries.shape[1]
    span = source_cache.shape[3]
    adopt = source_cache.shape[1] * n_tp
    res_rows = resident_cache.shape[2]
    per_dev = queries.shape[2] // HD
    group = QH // KVH
    kv_dev = max(1, per_dev // group)
    per_kv = per_dev // kv_dev
    wide = kv_dev * HD
    depth, model = out_weight.shape
    pieces = pieces_of(rows)
    stack = (rows * pieces, model // n_tp // pieces)
    dims = (n_inst, n_tp, adopt, res_rows, kv_dev, per_kv, span)
    dma = pltpu.SemaphoreType.DMA
    any_spec = pl.BlockSpec(memory_space=pl.ANY)
    mixed, adopted = pl.pallas_call(
        functools.partial(kernel, dims),
        out_shape=(
            jax.ShapeDtypeStruct((rows, model), BF16),
            jax.ShapeDtypeStruct((1, 1, adopt, 2, span, wide), BF16),
        ),
        in_specs=[pl.BlockSpec(memory_space=pltpu.HBM)] * 7,
        out_specs=(any_spec, any_spec),
        scratch_shapes=[
            pltpu.VMEM(source_cache.shape, BF16),
            pltpu.VMEM((adopt, 2, span, wide), BF16),
            pltpu.VMEM(resident_cache.shape, BF16),
            pltpu.VMEM(out_weight.shape, BF16),
            pltpu.VMEM(queries.shape, BF16),
            pltpu.VMEM(new_kv.shape, BF16),
            pltpu.VMEM(residual.shape, BF16),
            pltpu.VMEM(lengths.shape, jnp.int32),
            pltpu.VMEM(queries.shape[1:], F32),
            pltpu.VMEM((rows, per_dev, HD), F32),
            pltpu.VMEM((n_tp, per_dev, HD), F32),
            pltpu.VMEM((rows, 2, wide), F32),
            pltpu.VMEM(new_kv.shape[2:], F32),
            pltpu.VMEM(new_kv.shape[2:], F32),
            pltpu.VMEM((rows, model), F32),
            pltpu.VMEM((n_tp, per_dev, HD), F32),
            pltpu.VMEM((adopt, per_dev, HD), F32),
            pltpu.VMEM((rows, depth), F32),
            pltpu.VMEM((n_tp,) + stack, BF16),
            pltpu.VMEM((n_tp,) + stack, BF16),
            pltpu.VMEM((n_tp,) + stack, BF16),
            pltpu.VMEM(stack, F32),
            pltpu.VMEM((rows, model), BF16),
            dma((4, n_tp)),
            dma((4, n_tp)),
            dma((4, n_tp)),
            dma((8,)),
            dma((adopt,)),
            dma((n_tp,)),
            dma((2,)),
            dma((n_tp,)),
            dma((adopt,)),
        ]
        + [dma((n_tp,))] * 4,
        compiler_params=pltpu.CompilerParams(
            collective_id=0, has_side_effects=True, vmem_limit_bytes=60 * 1024 * 1024
        ),
        cost_estimate=pl.CostEstimate(
            flops=2 * rows * depth * model, bytes_accessed=2 * depth * model, transcendentals=0
        ),
        name="handoff_attention",
    )(source_cache, resident_cache, new_kv, queries, residual, lengths, out_weight)
    return pl.pallas_call(
        place_outputs,
        out_shape=(
            jax.ShapeDtypeStruct((1, rows, model), BF16),
            jax.ShapeDtypeStruct(adopted.shape, BF16),
        ),
        in_specs=[any_spec, any_spec],
        out_specs=(any_spec, any_spec),
        scratch_shapes=[
            pltpu.VMEM((rows, model), BF16),
            pltpu.VMEM((adopt, 2, span, wide), BF16),
            dma((1 + 2 * adopt,)),
            dma((1 + 2 * adopt,)),
        ],
        compiler_params=pltpu.CompilerParams(vmem_limit_bytes=60 * 1024 * 1024),
        cost_estimate=pl.CostEstimate(flops=0, bytes_accessed=4 * adopted.size, transcendentals=0),
        name="place_outputs",
    )(mixed, adopted)


def solution(mesh):
    in_specs = (
        P("inst", "tp", None, None, None),
        P("inst", "tp", None, None, None, None),
        P("inst", None, None, None),
        P("inst", None, "tp"),
        P("inst", None, None),
        P("inst", None),
        P("tp", None),
    )
    out_specs = (P("inst", None, None), P("inst", "tp", None, None, None, None))
    return jax.shard_map(
        functools.partial(on_device, mesh.shape["inst"], mesh.shape["tp"]),
        mesh=mesh, in_specs=in_specs, out_specs=out_specs, check_vma=False,
    )
```

```python
import functools
import math

import jax
import jax.numpy as jnp
from jax import lax
from jax.experimental import pallas as pl
from jax.experimental.pallas import tpu as pltpu
from jax.sharding import PartitionSpec as P

HD = 128
KVH = 8
QH = 32
TILE = 16
MESH = pl.DeviceIdType.MESH
BF16 = jnp.bfloat16
F32 = jnp.float32


def pieces_of(rows):
    return TILE // math.gcd(rows, TILE)


def kernel(
    dims,
    source_ref, resident_ref, newkv_ref, query_ref, resid_ref, lens_ref, weight_ref,
    mixed_ref, adopted_ref,
    source, cache, resident, weight, q_raw, nk_raw, rs_raw, len_raw,
    qf, q_rows, q_in, nkf, nk_out, nk_in, resf, o_out, o_in, attn,
    part_out, part_in, final, total, half_out, half_in, mixed,
    kv_send, kv_recv, keep_sem, load_sem, q_send, q_recv, nk_sem, o_send, o_recv,
    rs_send, rs_recv, ag_send, ag_recv, cross_sem,
):
    n_inst, n_tp, adopt, res_rows, kv_dev, per_kv, span = dims
    rows = adopt + res_rows
    per_dev = kv_dev * per_kv
    group = QH // KVH
    wide = kv_dev * HD
    inst, tp = lax.axis_index("inst"), lax.axis_index("tp")
    other = lax.rem(inst + n_inst // 2, n_inst)
    scale = 1.0 / math.sqrt(HD)
    model = weight_ref.shape[1]
    side = n_tp // 2
    near, mine = tp // side * side, lax.rem(tp, side)
    share = model // side
    pieces = pieces_of(rows)
    width = share // pieces

    def column(rank):
        return rank * per_dev // group * HD

    def my_columns(rank):
        return pl.ds(pl.multiple_of(column(rank), HD), wide)

    barrier = pltpu.get_barrier_semaphore()
    for o in range(n_tp):
        pl.semaphore_signal(barrier, inc=1, device_id=(other, lax.rem(tp + o, n_tp)), device_id_type=MESH)
        if o > 0:
            pl.semaphore_signal(barrier, inc=1, device_id=(inst, lax.rem(tp + o, n_tp)), device_id_type=MESH)
    loads = [
        pltpu.make_async_copy(src, dst, load_sem.at[j])
        for j, (src, dst) in enumerate(
            (
                (query_ref, q_raw),
                (newkv_ref, nk_raw),
                (lens_ref, len_raw),
                (source_ref, source),
                (resident_ref, resident),
                (resid_ref, rs_raw),
                (weight_ref, weight),
            )
        )
    ]
    for load in loads[:4]:
        load.start()
    pl.semaphore_wait(barrier, 2 * n_tp - 1)

    core = lax.rem(inst, 2)

    half = span // 2

    def handoff(j):
        phase, k = j // n_tp, j % n_tp
        which, piece = phase // 2, phase % 2
        base = (k // 2 + (n_tp // 2 if k % 2 == 0 else 0)) % n_tp
        rank = lax.rem(tp + base + core * (n_tp // 2), n_tp)
        rows_of = pl.ds(piece * half, half)
        return pltpu.make_async_remote_copy(
            src_ref=source.at[0, 0, which, rows_of, my_columns(rank)],
            dst_ref=cache.at[tp, which, rows_of],
            send_sem=kv_send.at[phase, k],
            recv_sem=kv_recv.at[phase, tp],
            device_id=(other, rank),
            device_id_type=MESH,
        )

    def keep(j):
        phase, k = j // n_tp, j % n_tp
        which, rows_of = phase // 2, pl.ds(phase % 2 * half, half)
        return pltpu.make_async_copy(
            cache.at[k, which, rows_of], adopted_ref.at[0, 0, k, which, rows_of], keep_sem.at[phase, k]
        )

    def start_handoff(first, last):
        for j in range(first * n_tp // 4, last * n_tp // 4):
            handoff(j).start()

    def send(src, dst, send_sem, recv_sem, device):
        return pltpu.make_async_remote_copy(
            src_ref=src, dst_ref=dst, send_sem=send_sem, recv_sem=recv_sem,
            device_id=device, device_id_type=MESH,
        )

    loads[3].wait()
    start_handoff(0, 2)
    for load in loads[4:]:
        load.start()
    for load in loads[:3]:
        load.wait()

    def rows_to_heads(first, last):
        for row in range(first, last):
            q_rows[row] = jnp.concatenate(
                [qf[row : row + 1, h * HD : (h + 1) * HD] for h in range(per_dev)], axis=0
            )

    qf[...] = q_raw[0].astype(F32)
    nk_out[...] = nk_raw[0, tp].astype(F32)
    rows_to_heads(0, adopt)
    q_sends = [
        send(q_rows.at[r], q_in.at[tp], q_send.at[r], q_recv.at[tp], (other, r)) for r in range(adopt)
    ]
    nk_send = send(nk_out, nk_in, nk_sem.at[0], nk_sem.at[1], (other, tp))
    for copy in q_sends:
        copy.start()
    nk_send.start()
    start_handoff(2, 6)
    rows_to_heads(adopt, rows)
    nkf[...] = nk_raw[0, :, :, my_columns(tp)].astype(F32)

    head = lax.broadcasted_iota(jnp.int32, (per_dev, HD), 0)
    place = lax.broadcasted_iota(jnp.int32, (per_dev, span), 1)

    def attention(q, keys, values, own_key, own_value, length):
        spread = jnp.concatenate(
            [jnp.where(head // per_kv == s, q, 0.0) for s in range(kv_dev)], axis=1
        )
        score = lax.dot_general(
            spread.astype(BF16), keys, (((1,), (1,)), ((), ())), preferred_element_type=F32
        ) * scale
        own = jnp.sum(spread * own_key, axis=1, keepdims=True) * scale
        live = place < length
        score = jnp.where(live, score, -1e30)
        top = jnp.maximum(jnp.max(score, axis=1, keepdims=True), own)
        part = jnp.where(live, jnp.exp(score - top), 0.0)
        own_part = jnp.exp(own - top)
        whole = jnp.sum(part, axis=1, keepdims=True) + own_part
        p = (part / whole).astype(BF16)
        own_p = (own_part / whole).astype(BF16).astype(F32)
        o = jnp.dot(p, values, preferred_element_type=F32) + own_p * own_value
        result = o[:, 0:HD]
        for s in range(1, kv_dev):
            result = jnp.where(head // per_kv == s, o[:, s * HD : (s + 1) * HD], result)
        return result

    def place_row(row, heads):
        for h in range(per_dev):
            attn[row : row + 1, h * HD : (h + 1) * HD] = heads[h : h + 1, :]

    lens = len_raw[...]
    lane = lax.broadcasted_iota(jnp.int32, lens.shape, 1)
    handed = jnp.sum(jnp.where(lane == tp, lens, 0), axis=1, keepdims=True)

    def serve(row):
        r = row - adopt
        place_row(
            row,
            attention(
                q_rows[row], resident[0, 0, r, 0], resident[0, 0, r, 1],
                nkf[row, 0:1, :], nkf[row, 1:2, :], lens[:, row : row + 1],
            ),
        )

    loads[4].wait()
    for row in range(adopt, adopt + res_rows // 2):
        serve(row)

    nk_send.wait_recv()
    for rank in range(n_tp):
        send(q_rows.at[rank], q_in.at[rank], q_send.at[rank], q_recv.at[rank], (other, rank)).wait_recv()
    o_sends = []
    for rank in range(n_tp):
        at = column(rank)
        o_out[rank] = attention(
            q_in[rank], source[0, 0, 0, :, at : at + wide], source[0, 0, 1, :, at : at + wide],
            nk_in[0:1, at : at + wide], nk_in[1:2, at : at + wide], handed,
        )
        copy = send(o_out.at[rank], o_in.at[tp], o_send.at[rank], o_recv.at[tp], (other, rank))
        copy.start()
        o_sends.append(copy)
    start_handoff(6, 10)

    for row in range(adopt + res_rows // 2, rows):
        serve(row)
    loads[5].wait()
    resf[...] = rs_raw[0].astype(F32)
    for row in range(adopt):
        send(o_out.at[row], o_in.at[row], o_send.at[row], o_recv.at[row], (other, row)).wait_recv()
        place_row(row, o_in[row])
    loads[6].wait()

    def project(part):
        a = attn[...].astype(BF16)
        parts = []
        for j in range(pieces):
            at = pl.multiple_of(part * share + j * width, HD)
            parts.append(jnp.dot(a, weight[:, pl.ds(at, width)], preferred_element_type=F32))
        return jnp.concatenate(parts, axis=0)

    @pl.loop(1, side)
    def _(o):
        part = lax.rem(mine + o, side)
        part_out[o] = project(part).astype(BF16)
        send(part_out.at[o], part_in.at[mine], rs_send.at[o], rs_recv.at[mine], (inst, near + part)).start()

    start_handoff(10, 12)
    total[...] = project(mine)
    for o in range(1, side):
        part = lax.rem(mine + o, side)
        send(part_out.at[o], part_in.at[part], rs_send.at[o], rs_recv.at[part], (inst, near + part)).wait_recv()
        total[...] += part_in[part].astype(F32)

    half_out[...] = total[...].astype(BF16)
    cross = send(
        half_out, half_in, cross_sem.at[0], cross_sem.at[1], (inst, lax.rem(tp + side, n_tp))
    )
    cross.start()
    start_handoff(12, 14)
    cross.wait_recv()
    extra = jnp.concatenate(
        [
            resf[:, pl.ds(pl.multiple_of(mine * share + j * width, HD), width)]
            for j in range(pieces)
        ],
        axis=0,
    )
    final[mine] = (half_out[...].astype(F32) + half_in[...].astype(F32) + extra).astype(BF16)

    def give(o):
        part = lax.rem(mine + o, side)
        return send(final.at[mine], final.at[mine], ag_send.at[o], ag_recv.at[mine], (inst, near + part))

    for o in range(1, side):
        give(o).start()
    start_handoff(14, 16)
    for o in range(1, side):
        part = lax.rem(mine + o, side)
        send(final.at[part], final.at[part], ag_send.at[o], ag_recv.at[part], (inst, near + part)).wait_recv()
    for part in range(side):
        block = final[part].astype(F32)
        for j in range(pieces):
            at = part * share + j * width
            mixed[:, at : at + width] = block[j * rows : (j + 1) * rows].astype(BF16)
    mixed_copy = pltpu.make_async_copy(mixed, mixed_ref, load_sem.at[7])
    mixed_copy.start()

    mixed_copy.wait()
    for copy in q_sends:
        copy.wait_send()
    nk_send.wait_send()
    for copy in o_sends:
        copy.wait_send()
    cross.wait_send()
    for o in range(1, side):
        part = lax.rem(mine + o, side)
        send(part_out.at[o], part_in.at[mine], rs_send.at[o], rs_recv.at[mine], (inst, near + part)).wait_send()
        give(o).wait_send()
    for j in range(4 * n_tp):
        handoff(j).wait_send()
        phase, k = j // n_tp, j % n_tp
        rows_of = pl.ds(phase % 2 * half, half)
        there = cache.at[k, phase // 2, rows_of]
        send(there, there, kv_send.at[phase, k], kv_recv.at[phase, k], (other, k)).wait_recv()
        keep(j).start()
    for j in range(4 * n_tp):
        keep(j).wait()


def place_outputs(mixed_ref, adopted_ref, mixed_out, adopted_out, mixed, cache, load_sem, store_sem):
    loads = [pltpu.make_async_copy(mixed_ref, mixed, load_sem.at[0])]
    stores = [pltpu.make_async_copy(mixed, mixed_out.at[0], store_sem.at[0])]
    for row in range(adopted_ref.shape[2]):
        for which in range(2):
            at = 1 + 2 * row + which
            there = cache.at[row, which]
            loads.append(pltpu.make_async_copy(adopted_ref.at[0, 0, row, which], there, load_sem.at[at]))
            stores.append(pltpu.make_async_copy(there, adopted_out.at[0, 0, row, which], store_sem.at[at]))
    for load in loads:
        load.start()
    for load, store in zip(loads, stores):
        load.wait()
        store.start()
    for store in stores:
        store.wait()


def on_device(n_inst, n_tp, source_cache, resident_cache, new_kv, queries, residual, lengths, out_weight):
    rows = queries.shape[1]
    span = source_cache.shape[3]
    adopt = source_cache.shape[1] * n_tp
    res_rows = resident_cache.shape[2]
    per_dev = queries.shape[2] // HD
    group = QH // KVH
    kv_dev = max(1, per_dev // group)
    per_kv = per_dev // kv_dev
    wide = kv_dev * HD
    depth, model = out_weight.shape
    pieces = pieces_of(rows)
    side = n_tp // 2
    stack = (rows * pieces, model // side // pieces)
    dims = (n_inst, n_tp, adopt, res_rows, kv_dev, per_kv, span)
    dma = pltpu.SemaphoreType.DMA
    any_spec = pl.BlockSpec(memory_space=pl.ANY)
    mixed, adopted = pl.pallas_call(
        functools.partial(kernel, dims),
        out_shape=(
            jax.ShapeDtypeStruct((rows, model), BF16),
            jax.ShapeDtypeStruct((1, 1, adopt, 2, span, wide), BF16),
        ),
        in_specs=[pl.BlockSpec(memory_space=pltpu.HBM)] * 7,
        out_specs=(any_spec, any_spec),
        scratch_shapes=[
            pltpu.VMEM(source_cache.shape, BF16),
            pltpu.VMEM((adopt, 2, span, wide), BF16),
            pltpu.VMEM(resident_cache.shape, BF16),
            pltpu.VMEM(out_weight.shape, BF16),
            pltpu.VMEM(queries.shape, BF16),
            pltpu.VMEM(new_kv.shape, BF16),
            pltpu.VMEM(residual.shape, BF16),
            pltpu.VMEM(lengths.shape, jnp.int32),
            pltpu.VMEM(queries.shape[1:], F32),
            pltpu.VMEM((rows, per_dev, HD), F32),
            pltpu.VMEM((n_tp, per_dev, HD), F32),
            pltpu.VMEM((rows, 2, wide), F32),
            pltpu.VMEM(new_kv.shape[2:], F32),
            pltpu.VMEM(new_kv.shape[2:], F32),
            pltpu.VMEM((rows, model), F32),
            pltpu.VMEM((n_tp, per_dev, HD), F32),
            pltpu.VMEM((adopt, per_dev, HD), F32),
            pltpu.VMEM((rows, depth), F32),
            pltpu.VMEM((side,) + stack, BF16),
            pltpu.VMEM((side,) + stack, BF16),
            pltpu.VMEM((side,) + stack, BF16),
            pltpu.VMEM(stack, F32),
            pltpu.VMEM(stack, BF16),
            pltpu.VMEM(stack, BF16),
            pltpu.VMEM((rows, model), BF16),
            dma((4, n_tp)),
            dma((4, n_tp)),
            dma((4, n_tp)),
            dma((8,)),
            dma((adopt,)),
            dma((n_tp,)),
            dma((2,)),
            dma((n_tp,)),
            dma((adopt,)),
        ]
        + [dma((side,))] * 4
        + [dma((2,))],
        compiler_params=pltpu.CompilerParams(
            collective_id=0, has_side_effects=True, vmem_limit_bytes=60 * 1024 * 1024
        ),
        cost_estimate=pl.CostEstimate(
            flops=2 * rows * depth * model, bytes_accessed=2 * depth * model, transcendentals=0
        ),
        name="handoff_attention",
    )(source_cache, resident_cache, new_kv, queries, residual, lengths, out_weight)
    return pl.pallas_call(
        place_outputs,
        out_shape=(
            jax.ShapeDtypeStruct((1, rows, model), BF16),
            jax.ShapeDtypeStruct(adopted.shape, BF16),
        ),
        in_specs=[any_spec, any_spec],
        out_specs=(any_spec, any_spec),
        scratch_shapes=[
            pltpu.VMEM((rows, model), BF16),
            pltpu.VMEM((adopt, 2, span, wide), BF16),
            dma((1 + 2 * adopt,)),
            dma((1 + 2 * adopt,)),
        ],
        compiler_params=pltpu.CompilerParams(vmem_limit_bytes=60 * 1024 * 1024),
        cost_estimate=pl.CostEstimate(flops=0, bytes_accessed=4 * adopted.size, transcendentals=0),
        name="place_outputs",
    )(mixed, adopted)


def solution(mesh):
    in_specs = (
        P("inst", "tp", None, None, None),
        P("inst", "tp", None, None, None, None),
        P("inst", None, None, None),
        P("inst", None, "tp"),
        P("inst", None, None),
        P("inst", None),
        P("tp", None),
    )
    out_specs = (P("inst", None, None), P("inst", "tp", None, None, None, None))
    return jax.shard_map(
        functools.partial(on_device, mesh.shape["inst"], mesh.shape["tp"]),
        mesh=mesh, in_specs=in_specs, out_specs=out_specs, check_vma=False,
    )
```

```python
import functools
import math

import jax
import jax.numpy as jnp
from jax import lax
from jax.experimental import pallas as pl
from jax.experimental.pallas import tpu as pltpu
from jax.sharding import PartitionSpec as P

HD = 128
KVH = 8
QH = 32
TILE = 16
MESH = pl.DeviceIdType.MESH
BF16 = jnp.bfloat16
F32 = jnp.float32


def pieces_of(rows):
    return TILE // math.gcd(rows, TILE)


def kernel(
    dims,
    source_ref, resident_ref, newkv_ref, query_ref, resid_ref, lens_ref, weight_ref,
    mixed_ref, adopted_ref,
    source, cache, resident, weight, q_raw, nk_raw, rs_raw, len_raw,
    qf, q_rows, q_in, nkf, nk_out, nk_in, resf, o_out, o_in, attn,
    part_out, part_in, final, total, half_out, half_in, mixed,
    kv_send, kv_recv, keep_sem, load_sem, q_send, q_recv, nk_sem, o_send, o_recv,
    rs_send, rs_recv, ag_send, ag_recv, cross_sem,
):
    n_inst, n_tp, adopt, res_rows, kv_dev, per_kv, span = dims
    rows = adopt + res_rows
    per_dev = kv_dev * per_kv
    group = QH // KVH
    wide = kv_dev * HD
    inst, tp = lax.axis_index("inst"), lax.axis_index("tp")
    other = lax.rem(inst + n_inst // 2, n_inst)
    scale = 1.0 / math.sqrt(HD)
    model = weight_ref.shape[1]
    side = n_tp // 2
    near, mine = tp // side * side, lax.rem(tp, side)
    share = model // side
    pieces = pieces_of(rows)
    width = share // pieces

    def column(rank):
        return rank * per_dev // group * HD

    def my_columns(rank):
        return pl.ds(pl.multiple_of(column(rank), HD), wide)

    barrier = pltpu.get_barrier_semaphore()
    for o in range(n_tp):
        pl.semaphore_signal(barrier, inc=1, device_id=(other, lax.rem(tp + o, n_tp)), device_id_type=MESH)
        if o > 0:
            pl.semaphore_signal(barrier, inc=1, device_id=(inst, lax.rem(tp + o, n_tp)), device_id_type=MESH)
    loads = [
        pltpu.make_async_copy(src, dst, load_sem.at[j])
        for j, (src, dst) in enumerate(
            (
                (query_ref, q_raw),
                (newkv_ref, nk_raw),
                (lens_ref, len_raw),
                (source_ref, source),
                (resident_ref, resident),
                (resid_ref, rs_raw),
                (weight_ref, weight),
            )
        )
    ]
    for load in loads[:4]:
        load.start()
    pl.semaphore_wait(barrier, 2 * n_tp - 1)

    core = lax.rem(inst, 2)

    half = span // 2

    def handoff(j):
        phase, k = j // n_tp, j % n_tp
        which, piece = phase // 2, phase % 2
        base = (k // 2 + (n_tp // 2 if k % 2 == 0 else 0)) % n_tp
        rank = lax.rem(tp + base + core * (n_tp // 2), n_tp)
        rows_of = pl.ds(piece * half, half)
        return pltpu.make_async_remote_copy(
            src_ref=source.at[0, 0, which, rows_of, my_columns(rank)],
            dst_ref=cache.at[tp, which, rows_of],
            send_sem=kv_send.at[phase, k],
            recv_sem=kv_recv.at[phase, tp],
            device_id=(other, rank),
            device_id_type=MESH,
        )

    def keep(j):
        phase, k = j // n_tp, j % n_tp
        which, rows_of = phase // 2, pl.ds(phase % 2 * half, half)
        return pltpu.make_async_copy(
            cache.at[k, which, rows_of], adopted_ref.at[0, 0, k, which, rows_of], keep_sem.at[phase, k]
        )

    def start_handoff(first, last):
        for j in range(first * n_tp // 4, last * n_tp // 4):
            handoff(j).start()

    def send(src, dst, send_sem, recv_sem, device):
        return pltpu.make_async_remote_copy(
            src_ref=src, dst_ref=dst, send_sem=send_sem, recv_sem=recv_sem,
            device_id=device, device_id_type=MESH,
        )

    loads[3].wait()
    start_handoff(0, 2)
    for load in loads[4:]:
        load.start()
    for load in loads[:3]:
        load.wait()

    def rows_to_heads(first, last):
        for row in range(first, last):
            q_rows[row] = jnp.concatenate(
                [qf[row : row + 1, h * HD : (h + 1) * HD] for h in range(per_dev)], axis=0
            )

    qf[...] = q_raw[0].astype(F32)
    nk_out[...] = nk_raw[0, tp].astype(F32)
    rows_to_heads(0, adopt)
    q_sends = [
        send(q_rows.at[r], q_in.at[tp], q_send.at[r], q_recv.at[tp], (other, r)) for r in range(adopt)
    ]
    nk_send = send(nk_out, nk_in, nk_sem.at[0], nk_sem.at[1], (other, tp))
    for copy in q_sends:
        copy.start()
    nk_send.start()
    start_handoff(2, 6)
    rows_to_heads(adopt, rows)
    nkf[...] = nk_raw[0, :, :, my_columns(tp)].astype(F32)

    head = lax.broadcasted_iota(jnp.int32, (per_dev, HD), 0)
    place = lax.broadcasted_iota(jnp.int32, (per_dev, span), 1)

    def attention(q, keys, values, own_key, own_value, length):
        spread = jnp.concatenate(
            [jnp.where(head // per_kv == s, q, 0.0) for s in range(kv_dev)], axis=1
        )
        score = lax.dot_general(
            spread.astype(BF16), keys, (((1,), (1,)), ((), ())), preferred_element_type=F32
        ) * scale
        own = jnp.sum(spread * own_key, axis=1, keepdims=True) * scale
        live = place < length
        score = jnp.where(live, score, -1e30)
        top = jnp.maximum(jnp.max(score, axis=1, keepdims=True), own)
        part = jnp.where(live, jnp.exp(score - top), 0.0)
        own_part = jnp.exp(own - top)
        whole = jnp.sum(part, axis=1, keepdims=True) + own_part
        p = (part / whole).astype(BF16)
        own_p = (own_part / whole).astype(BF16).astype(F32)
        o = jnp.dot(p, values, preferred_element_type=F32) + own_p * own_value
        result = o[:, 0:HD]
        for s in range(1, kv_dev):
            result = jnp.where(head // per_kv == s, o[:, s * HD : (s + 1) * HD], result)
        return result

    def place_row(row, heads):
        for h in range(per_dev):
            attn[row : row + 1, h * HD : (h + 1) * HD] = heads[h : h + 1, :]

    lens = len_raw[...]
    lane = lax.broadcasted_iota(jnp.int32, lens.shape, 1)
    handed = jnp.sum(jnp.where(lane == tp, lens, 0), axis=1, keepdims=True)

    def serve(row):
        r = row - adopt
        place_row(
            row,
            attention(
                q_rows[row], resident[0, 0, r, 0], resident[0, 0, r, 1],
                nkf[row, 0:1, :], nkf[row, 1:2, :], lens[:, row : row + 1],
            ),
        )

    loads[4].wait()
    for row in range(adopt, adopt + res_rows // 2):
        serve(row)

    nk_send.wait_recv()
    for rank in range(n_tp):
        send(q_rows.at[rank], q_in.at[rank], q_send.at[rank], q_recv.at[rank], (other, rank)).wait_recv()
    o_sends = []
    for rank in range(n_tp):
        at = column(rank)
        o_out[rank] = attention(
            q_in[rank], source[0, 0, 0, :, at : at + wide], source[0, 0, 1, :, at : at + wide],
            nk_in[0:1, at : at + wide], nk_in[1:2, at : at + wide], handed,
        )
        copy = send(o_out.at[rank], o_in.at[tp], o_send.at[rank], o_recv.at[tp], (other, rank))
        copy.start()
        o_sends.append(copy)
    start_handoff(6, 11)

    for row in range(adopt + res_rows // 2, rows):
        serve(row)
    loads[5].wait()
    resf[...] = rs_raw[0].astype(F32)
    for row in range(adopt):
        send(o_out.at[row], o_in.at[row], o_send.at[row], o_recv.at[row], (other, row)).wait_recv()
        place_row(row, o_in[row])
    loads[6].wait()

    def project(part):
        a = attn[...].astype(BF16)
        parts = []
        for j in range(pieces):
            at = pl.multiple_of(part * share + j * width, HD)
            parts.append(jnp.dot(a, weight[:, pl.ds(at, width)], preferred_element_type=F32))
        return jnp.concatenate(parts, axis=0)

    @pl.loop(1, side)
    def _(o):
        part = lax.rem(mine + o, side)
        part_out[o] = project(part).astype(BF16)
        send(part_out.at[o], part_in.at[mine], rs_send.at[o], rs_recv.at[mine], (inst, near + part)).start()

    start_handoff(11, 14)
    total[...] = project(mine)
    for o in range(1, side):
        part = lax.rem(mine + o, side)
        send(part_out.at[o], part_in.at[part], rs_send.at[o], rs_recv.at[part], (inst, near + part)).wait_recv()
        total[...] += part_in[part].astype(F32)

    half_out[...] = total[...].astype(BF16)
    cross = send(
        half_out, half_in, cross_sem.at[0], cross_sem.at[1], (inst, lax.rem(tp + side, n_tp))
    )
    cross.start()
    start_handoff(14, 16)
    cross.wait_recv()
    extra = jnp.concatenate(
        [
            resf[:, pl.ds(pl.multiple_of(mine * share + j * width, HD), width)]
            for j in range(pieces)
        ],
        axis=0,
    )
    final[mine] = (half_out[...].astype(F32) + half_in[...].astype(F32) + extra).astype(BF16)

    def give(o):
        part = lax.rem(mine + o, side)
        return send(final.at[mine], final.at[mine], ag_send.at[o], ag_recv.at[mine], (inst, near + part))

    for o in range(1, side):
        give(o).start()
    for o in range(1, side):
        part = lax.rem(mine + o, side)
        send(final.at[part], final.at[part], ag_send.at[o], ag_recv.at[part], (inst, near + part)).wait_recv()
    for part in range(side):
        block = final[part].astype(F32)
        for j in range(pieces):
            at = part * share + j * width
            mixed[:, at : at + width] = block[j * rows : (j + 1) * rows].astype(BF16)
    mixed_copy = pltpu.make_async_copy(mixed, mixed_ref, load_sem.at[7])
    mixed_copy.start()

    mixed_copy.wait()
    for copy in q_sends:
        copy.wait_send()
    nk_send.wait_send()
    for copy in o_sends:
        copy.wait_send()
    cross.wait_send()
    for o in range(1, side):
        part = lax.rem(mine + o, side)
        send(part_out.at[o], part_in.at[mine], rs_send.at[o], rs_recv.at[mine], (inst, near + part)).wait_send()
        give(o).wait_send()
    for j in range(4 * n_tp):
        handoff(j).wait_send()
        phase, k = j // n_tp, j % n_tp
        rows_of = pl.ds(phase % 2 * half, half)
        there = cache.at[k, phase // 2, rows_of]
        send(there, there, kv_send.at[phase, k], kv_recv.at[phase, k], (other, k)).wait_recv()
        keep(j).start()
    for j in range(4 * n_tp):
        keep(j).wait()


def place_outputs(mixed_ref, adopted_ref, mixed_out, adopted_out, mixed, cache, load_sem, store_sem):
    loads = [pltpu.make_async_copy(mixed_ref, mixed, load_sem.at[0])]
    stores = [pltpu.make_async_copy(mixed, mixed_out.at[0], store_sem.at[0])]
    for row in range(adopted_ref.shape[2]):
        for which in range(2):
            at = 1 + 2 * row + which
            there = cache.at[row, which]
            loads.append(pltpu.make_async_copy(adopted_ref.at[0, 0, row, which], there, load_sem.at[at]))
            stores.append(pltpu.make_async_copy(there, adopted_out.at[0, 0, row, which], store_sem.at[at]))
    for load in loads:
        load.start()
    for load, store in zip(loads, stores):
        load.wait()
        store.start()
    for store in stores:
        store.wait()


def on_device(n_inst, n_tp, source_cache, resident_cache, new_kv, queries, residual, lengths, out_weight):
    rows = queries.shape[1]
    span = source_cache.shape[3]
    adopt = source_cache.shape[1] * n_tp
    res_rows = resident_cache.shape[2]
    per_dev = queries.shape[2] // HD
    group = QH // KVH
    kv_dev = max(1, per_dev // group)
    per_kv = per_dev // kv_dev
    wide = kv_dev * HD
    depth, model = out_weight.shape
    pieces = pieces_of(rows)
    side = n_tp // 2
    stack = (rows * pieces, model // side // pieces)
    dims = (n_inst, n_tp, adopt, res_rows, kv_dev, per_kv, span)
    dma = pltpu.SemaphoreType.DMA
    any_spec = pl.BlockSpec(memory_space=pl.ANY)
    mixed, adopted = pl.pallas_call(
        functools.partial(kernel, dims),
        out_shape=(
            jax.ShapeDtypeStruct((rows, model), BF16),
            jax.ShapeDtypeStruct((1, 1, adopt, 2, span, wide), BF16),
        ),
        in_specs=[pl.BlockSpec(memory_space=pltpu.HBM)] * 7,
        out_specs=(any_spec, any_spec),
        scratch_shapes=[
            pltpu.VMEM(source_cache.shape, BF16),
            pltpu.VMEM((adopt, 2, span, wide), BF16),
            pltpu.VMEM(resident_cache.shape, BF16),
            pltpu.VMEM(out_weight.shape, BF16),
            pltpu.VMEM(queries.shape, BF16),
            pltpu.VMEM(new_kv.shape, BF16),
            pltpu.VMEM(residual.shape, BF16),
            pltpu.VMEM(lengths.shape, jnp.int32),
            pltpu.VMEM(queries.shape[1:], F32),
            pltpu.VMEM((rows, per_dev, HD), F32),
            pltpu.VMEM((n_tp, per_dev, HD), F32),
            pltpu.VMEM((rows, 2, wide), F32),
            pltpu.VMEM(new_kv.shape[2:], F32),
            pltpu.VMEM(new_kv.shape[2:], F32),
            pltpu.VMEM((rows, model), F32),
            pltpu.VMEM((n_tp, per_dev, HD), F32),
            pltpu.VMEM((adopt, per_dev, HD), F32),
            pltpu.VMEM((rows, depth), F32),
            pltpu.VMEM((side,) + stack, BF16),
            pltpu.VMEM((side,) + stack, BF16),
            pltpu.VMEM((side,) + stack, BF16),
            pltpu.VMEM(stack, F32),
            pltpu.VMEM(stack, BF16),
            pltpu.VMEM(stack, BF16),
            pltpu.VMEM((rows, model), BF16),
            dma((4, n_tp)),
            dma((4, n_tp)),
            dma((4, n_tp)),
            dma((8,)),
            dma((adopt,)),
            dma((n_tp,)),
            dma((2,)),
            dma((n_tp,)),
            dma((adopt,)),
        ]
        + [dma((side,))] * 4
        + [dma((2,))],
        compiler_params=pltpu.CompilerParams(
            collective_id=0, has_side_effects=True, vmem_limit_bytes=60 * 1024 * 1024
        ),
        cost_estimate=pl.CostEstimate(
            flops=2 * rows * depth * model, bytes_accessed=2 * depth * model, transcendentals=0
        ),
        name="handoff_attention",
    )(source_cache, resident_cache, new_kv, queries, residual, lengths, out_weight)
    return pl.pallas_call(
        place_outputs,
        out_shape=(
            jax.ShapeDtypeStruct((1, rows, model), BF16),
            jax.ShapeDtypeStruct(adopted.shape, BF16),
        ),
        in_specs=[any_spec, any_spec],
        out_specs=(any_spec, any_spec),
        scratch_shapes=[
            pltpu.VMEM((rows, model), BF16),
            pltpu.VMEM((adopt, 2, span, wide), BF16),
            dma((1 + 2 * adopt,)),
            dma((1 + 2 * adopt,)),
        ],
        compiler_params=pltpu.CompilerParams(vmem_limit_bytes=60 * 1024 * 1024),
        cost_estimate=pl.CostEstimate(flops=0, bytes_accessed=4 * adopted.size, transcendentals=0),
        name="place_outputs",
    )(mixed, adopted)


def solution(mesh):
    in_specs = (
        P("inst", "tp", None, None, None),
        P("inst", "tp", None, None, None, None),
        P("inst", None, None, None),
        P("inst", None, "tp"),
        P("inst", None, None),
        P("inst", None),
        P("tp", None),
    )
    out_specs = (P("inst", None, None), P("inst", "tp", None, None, None, None))
    return jax.shard_map(
        functools.partial(on_device, mesh.shape["inst"], mesh.shape["tp"]),
        mesh=mesh, in_specs=in_specs, out_specs=out_specs, check_vma=False,
    )
```

```python
import functools
import math

import jax
import jax.numpy as jnp
from jax import lax
from jax.experimental import pallas as pl
from jax.experimental.pallas import tpu as pltpu
from jax.sharding import PartitionSpec as P

HD = 128
KVH = 8
QH = 32
TILE = 16
MESH = pl.DeviceIdType.MESH
BF16 = jnp.bfloat16
F32 = jnp.float32


def pieces_of(rows):
    return TILE // math.gcd(rows, TILE)


def kernel(
    dims,
    source_ref, resident_ref, newkv_ref, query_ref, resid_ref, lens_ref, weight_ref,
    mixed_ref, adopted_ref,
    source, cache, resident, weight, q_raw, nk_raw, rs_raw, len_raw,
    qf, q_rows, q_in, nkf, nk_out, nk_in, resf, o_out, o_in, attn,
    part_out, part_in, final, total, half_out, half_in, mixed,
    kv_send, kv_recv, keep_sem, load_sem, q_send, q_recv, nk_sem, o_send, o_recv,
    rs_send, rs_recv, ag_send, ag_recv, cross_sem,
):
    n_inst, n_tp, adopt, res_rows, kv_dev, per_kv, span = dims
    rows = adopt + res_rows
    per_dev = kv_dev * per_kv
    group = QH // KVH
    wide = kv_dev * HD
    inst, tp = lax.axis_index("inst"), lax.axis_index("tp")
    other = lax.rem(inst + n_inst // 2, n_inst)
    scale = 1.0 / math.sqrt(HD)
    model = weight_ref.shape[1]
    side = n_tp // 2
    near, mine = tp // side * side, lax.rem(tp, side)
    share = model // side
    pieces = pieces_of(rows)
    width = share // pieces

    def column(rank):
        return rank * per_dev // group * HD

    def my_columns(rank):
        return pl.ds(pl.multiple_of(column(rank), HD), wide)

    barrier = pltpu.get_barrier_semaphore()
    for o in range(n_tp):
        pl.semaphore_signal(barrier, inc=1, device_id=(other, lax.rem(tp + o, n_tp)), device_id_type=MESH)
        if o > 0:
            pl.semaphore_signal(barrier, inc=1, device_id=(inst, lax.rem(tp + o, n_tp)), device_id_type=MESH)
    loads = [
        pltpu.make_async_copy(src, dst, load_sem.at[j])
        for j, (src, dst) in enumerate(
            (
                (query_ref, q_raw),
                (newkv_ref, nk_raw),
                (lens_ref, len_raw),
                (source_ref, source),
                (resident_ref, resident),
                (resid_ref, rs_raw),
                (weight_ref, weight),
            )
        )
    ]
    for load in loads[:4]:
        load.start()
    for load in loads[:3]:
        load.wait()

    def rows_to_heads(first, last):
        for row in range(first, last):
            q_rows[row] = jnp.concatenate(
                [qf[row : row + 1, h * HD : (h + 1) * HD] for h in range(per_dev)], axis=0
            )

    qf[...] = q_raw[0].astype(F32)
    nk_out[...] = nk_raw[0, tp].astype(F32)
    rows_to_heads(0, adopt)
    pl.semaphore_wait(barrier, 2 * n_tp - 1)

    core = lax.rem(inst, 2)

    half = span // 2

    def handoff(j):
        phase, k = j // n_tp, j % n_tp
        which, piece = phase // 2, phase % 2
        base = (k // 2 + (n_tp // 2 if k % 2 == 0 else 0)) % n_tp
        rank = lax.rem(tp + base + core * (n_tp // 2), n_tp)
        rows_of = pl.ds(piece * half, half)
        return pltpu.make_async_remote_copy(
            src_ref=source.at[0, 0, which, rows_of, my_columns(rank)],
            dst_ref=cache.at[tp, which, rows_of],
            send_sem=kv_send.at[phase, k],
            recv_sem=kv_recv.at[phase, tp],
            device_id=(other, rank),
            device_id_type=MESH,
        )

    def keep(j):
        phase, k = j // n_tp, j % n_tp
        which, rows_of = phase // 2, pl.ds(phase % 2 * half, half)
        return pltpu.make_async_copy(
            cache.at[k, which, rows_of], adopted_ref.at[0, 0, k, which, rows_of], keep_sem.at[phase, k]
        )

    def start_handoff(first, last):
        for j in range(first * n_tp // 4, last * n_tp // 4):
            handoff(j).start()

    def send(src, dst, send_sem, recv_sem, device):
        return pltpu.make_async_remote_copy(
            src_ref=src, dst_ref=dst, send_sem=send_sem, recv_sem=recv_sem,
            device_id=device, device_id_type=MESH,
        )

    q_sends = [
        send(q_rows.at[r], q_in.at[tp], q_send.at[r], q_recv.at[tp], (other, r)) for r in range(adopt)
    ]
    nk_send = send(nk_out, nk_in, nk_sem.at[0], nk_sem.at[1], (other, tp))
    for copy in q_sends:
        copy.start()
    nk_send.start()
    loads[3].wait()
    start_handoff(0, 4)
    for load in loads[4:]:
        load.start()
    rows_to_heads(adopt, rows)
    nkf[...] = nk_raw[0, :, :, my_columns(tp)].astype(F32)

    head = lax.broadcasted_iota(jnp.int32, (per_dev, HD), 0)
    place = lax.broadcasted_iota(jnp.int32, (per_dev, span), 1)

    def attention(q, keys, values, own_key, own_value, length):
        spread = jnp.concatenate(
            [jnp.where(head // per_kv == s, q, 0.0) for s in range(kv_dev)], axis=1
        )
        score = lax.dot_general(
            spread.astype(BF16), keys, (((1,), (1,)), ((), ())), preferred_element_type=F32
        ) * scale
        own = jnp.sum(spread * own_key, axis=1, keepdims=True) * scale
        live = place < length
        score = jnp.where(live, score, -1e30)
        top = jnp.maximum(jnp.max(score, axis=1, keepdims=True), own)
        part = jnp.where(live, jnp.exp(score - top), 0.0)
        own_part = jnp.exp(own - top)
        whole = jnp.sum(part, axis=1, keepdims=True) + own_part
        p = (part / whole).astype(BF16)
        own_p = (own_part / whole).astype(BF16).astype(F32)
        o = jnp.dot(p, values, preferred_element_type=F32) + own_p * own_value
        result = o[:, 0:HD]
        for s in range(1, kv_dev):
            result = jnp.where(head // per_kv == s, o[:, s * HD : (s + 1) * HD], result)
        return result

    def place_row(row, heads):
        for h in range(per_dev):
            attn[row : row + 1, h * HD : (h + 1) * HD] = heads[h : h + 1, :]

    lens = len_raw[...]
    lane = lax.broadcasted_iota(jnp.int32, lens.shape, 1)
    handed = jnp.sum(jnp.where(lane == tp, lens, 0), axis=1, keepdims=True)

    def serve(row):
        r = row - adopt
        place_row(
            row,
            attention(
                q_rows[row], resident[0, 0, r, 0], resident[0, 0, r, 1],
                nkf[row, 0:1, :], nkf[row, 1:2, :], lens[:, row : row + 1],
            ),
        )

    loads[4].wait()
    for row in range(adopt, adopt + res_rows // 2):
        serve(row)

    nk_send.wait_recv()
    for rank in range(n_tp):
        send(q_rows.at[rank], q_in.at[rank], q_send.at[rank], q_recv.at[rank], (other, rank)).wait_recv()
    o_sends = []
    for rank in range(n_tp):
        at = column(rank)
        o_out[rank] = attention(
            q_in[rank], source[0, 0, 0, :, at : at + wide], source[0, 0, 1, :, at : at + wide],
            nk_in[0:1, at : at + wide], nk_in[1:2, at : at + wide], handed,
        )
        copy = send(o_out.at[rank], o_in.at[tp], o_send.at[rank], o_recv.at[tp], (other, rank))
        copy.start()
        o_sends.append(copy)
    start_handoff(4, 9)

    for row in range(adopt + res_rows // 2, rows):
        serve(row)
    loads[5].wait()
    resf[...] = rs_raw[0].astype(F32)
    for row in range(adopt):
        send(o_out.at[row], o_in.at[row], o_send.at[row], o_recv.at[row], (other, row)).wait_recv()
        place_row(row, o_in[row])
    loads[6].wait()

    def project(part):
        a = attn[...].astype(BF16)
        parts = []
        for j in range(pieces):
            at = pl.multiple_of(part * share + j * width, HD)
            parts.append(jnp.dot(a, weight[:, pl.ds(at, width)], preferred_element_type=F32))
        return jnp.concatenate(parts, axis=0)

    @pl.loop(1, side)
    def _(o):
        part = lax.rem(mine + o, side)
        part_out[o] = project(part).astype(BF16)
        send(part_out.at[o], part_in.at[mine], rs_send.at[o], rs_recv.at[mine], (inst, near + part)).start()

    start_handoff(9, 12)
    total[...] = project(mine)
    for o in range(1, side):
        part = lax.rem(mine + o, side)
        send(part_out.at[o], part_in.at[part], rs_send.at[o], rs_recv.at[part], (inst, near + part)).wait_recv()
        total[...] += part_in[part].astype(F32)

    half_out[...] = total[...].astype(BF16)
    cross = send(
        half_out, half_in, cross_sem.at[0], cross_sem.at[1], (inst, lax.rem(tp + side, n_tp))
    )
    cross.start()
    start_handoff(12, 14)
    cross.wait_recv()
    extra = jnp.concatenate(
        [
            resf[:, pl.ds(pl.multiple_of(mine * share + j * width, HD), width)]
            for j in range(pieces)
        ],
        axis=0,
    )
    final[mine] = (half_out[...].astype(F32) + half_in[...].astype(F32) + extra).astype(BF16)

    def give(o):
        part = lax.rem(mine + o, side)
        return send(final.at[mine], final.at[mine], ag_send.at[o], ag_recv.at[mine], (inst, near + part))

    for o in range(1, side):
        give(o).start()
    start_handoff(14, 16)
    for o in range(1, side):
        part = lax.rem(mine + o, side)
        send(final.at[part], final.at[part], ag_send.at[o], ag_recv.at[part], (inst, near + part)).wait_recv()
    for part in range(side):
        block = final[part].astype(F32)
        for j in range(pieces):
            at = part * share + j * width
            mixed[:, at : at + width] = block[j * rows : (j + 1) * rows].astype(BF16)
    mixed_copy = pltpu.make_async_copy(mixed, mixed_ref, load_sem.at[7])
    mixed_copy.start()

    mixed_copy.wait()
    for copy in q_sends:
        copy.wait_send()
    nk_send.wait_send()
    for copy in o_sends:
        copy.wait_send()
    cross.wait_send()
    for o in range(1, side):
        part = lax.rem(mine + o, side)
        send(part_out.at[o], part_in.at[mine], rs_send.at[o], rs_recv.at[mine], (inst, near + part)).wait_send()
        give(o).wait_send()
    for j in range(4 * n_tp):
        handoff(j).wait_send()
        phase, k = j // n_tp, j % n_tp
        rows_of = pl.ds(phase % 2 * half, half)
        there = cache.at[k, phase // 2, rows_of]
        send(there, there, kv_send.at[phase, k], kv_recv.at[phase, k], (other, k)).wait_recv()
        keep(j).start()
    for j in range(4 * n_tp):
        keep(j).wait()


def place_outputs(mixed_ref, adopted_ref, mixed_out, adopted_out, mixed, cache, load_sem, store_sem):
    loads = [pltpu.make_async_copy(mixed_ref, mixed, load_sem.at[0])]
    stores = [pltpu.make_async_copy(mixed, mixed_out.at[0], store_sem.at[0])]
    for row in range(adopted_ref.shape[2]):
        for which in range(2):
            at = 1 + 2 * row + which
            there = cache.at[row, which]
            loads.append(pltpu.make_async_copy(adopted_ref.at[0, 0, row, which], there, load_sem.at[at]))
            stores.append(pltpu.make_async_copy(there, adopted_out.at[0, 0, row, which], store_sem.at[at]))
    for load in loads:
        load.start()
    for load, store in zip(loads, stores):
        load.wait()
        store.start()
    for store in stores:
        store.wait()


def on_device(n_inst, n_tp, source_cache, resident_cache, new_kv, queries, residual, lengths, out_weight):
    rows = queries.shape[1]
    span = source_cache.shape[3]
    adopt = source_cache.shape[1] * n_tp
    res_rows = resident_cache.shape[2]
    per_dev = queries.shape[2] // HD
    group = QH // KVH
    kv_dev = max(1, per_dev // group)
    per_kv = per_dev // kv_dev
    wide = kv_dev * HD
    depth, model = out_weight.shape
    pieces = pieces_of(rows)
    side = n_tp // 2
    stack = (rows * pieces, model // side // pieces)
    dims = (n_inst, n_tp, adopt, res_rows, kv_dev, per_kv, span)
    dma = pltpu.SemaphoreType.DMA
    any_spec = pl.BlockSpec(memory_space=pl.ANY)
    mixed, adopted = pl.pallas_call(
        functools.partial(kernel, dims),
        out_shape=(
            jax.ShapeDtypeStruct((rows, model), BF16),
            jax.ShapeDtypeStruct((1, 1, adopt, 2, span, wide), BF16),
        ),
        in_specs=[pl.BlockSpec(memory_space=pltpu.HBM)] * 7,
        out_specs=(any_spec, any_spec),
        scratch_shapes=[
            pltpu.VMEM(source_cache.shape, BF16),
            pltpu.VMEM((adopt, 2, span, wide), BF16),
            pltpu.VMEM(resident_cache.shape, BF16),
            pltpu.VMEM(out_weight.shape, BF16),
            pltpu.VMEM(queries.shape, BF16),
            pltpu.VMEM(new_kv.shape, BF16),
            pltpu.VMEM(residual.shape, BF16),
            pltpu.VMEM(lengths.shape, jnp.int32),
            pltpu.VMEM(queries.shape[1:], F32),
            pltpu.VMEM((rows, per_dev, HD), F32),
            pltpu.VMEM((n_tp, per_dev, HD), F32),
            pltpu.VMEM((rows, 2, wide), F32),
            pltpu.VMEM(new_kv.shape[2:], F32),
            pltpu.VMEM(new_kv.shape[2:], F32),
            pltpu.VMEM((rows, model), F32),
            pltpu.VMEM((n_tp, per_dev, HD), F32),
            pltpu.VMEM((adopt, per_dev, HD), F32),
            pltpu.VMEM((rows, depth), F32),
            pltpu.VMEM((side,) + stack, BF16),
            pltpu.VMEM((side,) + stack, BF16),
            pltpu.VMEM((side,) + stack, BF16),
            pltpu.VMEM(stack, F32),
            pltpu.VMEM(stack, BF16),
            pltpu.VMEM(stack, BF16),
            pltpu.VMEM((rows, model), BF16),
            dma((4, n_tp)),
            dma((4, n_tp)),
            dma((4, n_tp)),
            dma((8,)),
            dma((adopt,)),
            dma((n_tp,)),
            dma((2,)),
            dma((n_tp,)),
            dma((adopt,)),
        ]
        + [dma((side,))] * 4
        + [dma((2,))],
        compiler_params=pltpu.CompilerParams(
            collective_id=0, has_side_effects=True, vmem_limit_bytes=60 * 1024 * 1024
        ),
        cost_estimate=pl.CostEstimate(
            flops=2 * rows * depth * model, bytes_accessed=2 * depth * model, transcendentals=0
        ),
        name="handoff_attention",
    )(source_cache, resident_cache, new_kv, queries, residual, lengths, out_weight)
    return pl.pallas_call(
        place_outputs,
        out_shape=(
            jax.ShapeDtypeStruct((1, rows, model), BF16),
            jax.ShapeDtypeStruct(adopted.shape, BF16),
        ),
        in_specs=[any_spec, any_spec],
        out_specs=(any_spec, any_spec),
        scratch_shapes=[
            pltpu.VMEM((rows, model), BF16),
            pltpu.VMEM((adopt, 2, span, wide), BF16),
            dma((1 + 2 * adopt,)),
            dma((1 + 2 * adopt,)),
        ],
        compiler_params=pltpu.CompilerParams(vmem_limit_bytes=60 * 1024 * 1024),
        cost_estimate=pl.CostEstimate(flops=0, bytes_accessed=4 * adopted.size, transcendentals=0),
        name="place_outputs",
    )(mixed, adopted)


def solution(mesh):
    in_specs = (
        P("inst", "tp", None, None, None),
        P("inst", "tp", None, None, None, None),
        P("inst", None, None, None),
        P("inst", None, "tp"),
        P("inst", None, None),
        P("inst", None),
        P("tp", None),
    )
    out_specs = (P("inst", None, None), P("inst", "tp", None, None, None, None))
    return jax.shard_map(
        functools.partial(on_device, mesh.shape["inst"], mesh.shape["tp"]),
        mesh=mesh, in_specs=in_specs, out_specs=out_specs, check_vma=False,
    )
```
